32 devices in a mesh: neur: 16 (over z, y, core), tm: 2 (over x).
Axes of the slice: x: 2, y: 2, z: 4, core: 2. Of those that a mesh axis runs over, the one named last changes fastest.
Arguments:
- spikes: int32 [512, 32768], P(None, ('neur', 'tm')), may hold values from 0 to 9
- held_in: int32 [32768], P(('neur', 'tm')), may hold values 0 or 1
- readin_weight: bfloat16 [32768, 1024], P(('neur', 'tm')), may hold values from -0.03125 to 0.03125
- qkv_weight: bfloat16 [1024, 3, 1024], P(None, None, 'tm'), may hold values from -0.1875 to 0.1875
- out_weight: bfloat16 [1024, 1024], P('tm'), may hold values from -0.1875 to 0.1875
- up_weight: bfloat16 [1024, 4096], P(None, 'tm'), may hold values from -0.1875 to 0.1875
- down_weight: bfloat16 [4096, 1024], P('tm'), may hold values from -0.09375 to 0.09375
- norm_gain: float32 [1024], replicated, may hold values from 0.25 to 1.75
- mlp_gain: float32 [1024], replicated, may hold values from 0.25 to 1.75
- final_gain: float32 [1024], replicated, may hold values from 0.25 to 1.75
- readout_weight: bfloat16 [32768, 1024], P(('neur', 'tm')), may hold values from -0.1875 to 0.1875
- readout_bias: float32 [32768], P(('neur', 'tm')), may hold values from -3 to 3
Outputs:
- latents: bfloat16 [512, 1024], P('neur')
- neuron_bits: float32 [32768], P(('neur', 'tm'))
- bits_per_spike: float32 [], replicated
The draws below stay inside these ranges and needn't reach their ends.
All inputs are finite; a program needn't handle non-finite values. No bound on the sum of `held_in` on one device may be relied on, other than what follows from the above.
Results may differ from the reference program's by a relative error of at most 0.006.
Values may be sent and summed in bfloat16 or wider, within the bound.
A program may use at most 64 MiB of HBM per device.

```python
import math
import jax
import jax.numpy as jnp
from jax import lax

D = 1024
HEADS = 8
HEAD_DIM = 128
FF = 4096
NEURONS = 32768
FRAMES = 512
N_NEUR = 16


def draw_spikes(key, part):
    key_ceiling, key_counts = jax.random.split(key)
    column = jnp.arange(NEURONS, dtype=jnp.int32)
    ceiling = 3 + 6 * column // NEURONS + jax.random.randint(key_ceiling, (NEURONS,), 0, 3)
    return jax.random.randint(key_counts, (FRAMES, NEURONS), 0, ceiling[None, :]).astype(jnp.int32)


def touch_ends(values, key, least, high):
    longest = values.shape.index(max(values.shape))
    spots = []
    for shift in (0, 1):
        where = [jax.random.randint(jax.random.fold_in(key, axis), (), 0, length) for axis, length in enumerate(values.shape)]
        where[longest] = (where[longest] + shift) % values.shape[longest]
        spots.append(tuple(where))
    return values.at[spots[0]].set(least).at[spots[1]].set(high)


def steps_of(stream_key, extent, cuts, smallest, top_value):
    level = 1.0
    for axis_at, parts in cuts:
        draws = jax.random.uniform(jax.random.fold_in(jax.random.fold_in(stream_key, 6), axis_at), (parts,), jnp.float32, smallest / len(cuts), top_value / len(cuts))
        level = level * jnp.repeat(jnp.exp(draws), extent[axis_at] // parts).reshape((-1,) + (1,) * (len(extent) - 1 - axis_at))
    return level


def bell_draw(stream_key, extent, width, reach, pieces=(), held_as=jnp.bfloat16):
    values = jax.random.normal(stream_key, extent, jnp.float32) * width
    if len(pieces) > 0:
        values = steps_of(stream_key, extent, pieces, -0.22, 0.18) * values
    return jnp.clip(values, min=-reach, max=reach).astype(held_as)


def setup_inputs(seed: int = 0) -> dict:
    keys = jax.random.split(jax.random.key(seed), 13)
    return {
        "spikes": draw_spikes(jax.random.fold_in(keys[12], 71), 0),
        "held_in": touch_ends((jax.random.randint(keys[1], (NEURONS,), 0, 2) < 1).astype(jnp.int32), jax.random.fold_in(keys[1], 1), 0, 1),
        "readin_weight": bell_draw(keys[2], (NEURONS, D), NEURONS ** -0.5, 0.03125, ((0, 32),)),
        "qkv_weight": bell_draw(keys[3], (D, 3, HEADS * HEAD_DIM), D ** -0.5, 0.1875, ((2, 2),)),
        "out_weight": bell_draw(keys[4], (HEADS * HEAD_DIM, D), (HEADS * HEAD_DIM) ** -0.5, 0.1875, ((0, 2),)),
        "up_weight": bell_draw(keys[5], (D, FF), D ** -0.5, 0.1875, ((1, 2),)),
        "down_weight": bell_draw(keys[6], (FF, D), FF ** -0.5, 0.09375, ((0, 2),)),
        "norm_gain": jnp.clip(1.0 + 0.15 * jax.random.normal(keys[7], (D,), jnp.float32), 0.25, 1.75),
        "mlp_gain": jnp.clip(1.0 + 0.15 * jax.random.normal(keys[8], (D,), jnp.float32), 0.25, 1.75),
        "final_gain": jnp.clip(1.0 + 0.15 * jax.random.normal(keys[9], (D,), jnp.float32), 0.25, 1.75),
        "readout_weight": bell_draw(keys[10], (NEURONS, D), D ** -0.5, 0.1875, ((0, 32),)),
        "readout_bias": bell_draw(keys[11], (NEURONS,), 0.5, 3.0, ((0, 32),), jnp.float32),
    }


def normed(values, gain_vec):
    return values * lax.rsqrt(lax.optimization_barrier(jnp.mean(values * values, -1, keepdims=True)) + 1e-05) * gain_vec

def reference(spikes, held_in, readin_weight, qkv_weight, out_weight, up_weight, down_weight, norm_gain, mlp_gain, final_gain, readout_weight, readout_bias):
    block_width = NEURONS // N_NEUR

    def readin_step(block_no, running):
        first_col = (block_no * block_width).astype(jnp.int32)
        cols = lax.dynamic_slice_in_dim(spikes, first_col, block_width, 1)
        mask_part = lax.dynamic_slice_in_dim(held_in, first_col, block_width, 0)
        masked = (cols * mask_part[None, :]).astype(jnp.bfloat16)
        rows_part = lax.dynamic_slice_in_dim(readin_weight, first_col, block_width, 0)
        return running + jnp.dot(masked, rows_part, preferred_element_type=jnp.float32)
    stream = lax.fori_loop(0, N_NEUR, readin_step, jnp.zeros((FRAMES, D), jnp.float32))
    attn_in = normed(stream, norm_gain).astype(jnp.bfloat16)
    head_cols = HEADS * HEAD_DIM
    projected = jnp.dot(attn_in, qkv_weight.reshape(D, 3 * head_cols), preferred_element_type=jnp.float32).astype(jnp.bfloat16)
    queries = projected[:, :head_cols].reshape(FRAMES, HEADS, HEAD_DIM).astype(jnp.float32)
    keys_all = projected[:, head_cols:2 * head_cols].reshape(FRAMES, HEADS, HEAD_DIM).astype(jnp.float32)
    values_all = projected[:, 2 * head_cols:].reshape(FRAMES, HEADS, HEAD_DIM).astype(jnp.float32)
    scores = jnp.einsum('qhd,khd->hqk', queries, keys_all) * (1.0 / math.sqrt(HEAD_DIM))
    weights = jnp.exp(scores)
    weights_low = weights.astype(jnp.bfloat16).astype(jnp.float32)
    numerator = jnp.einsum('hqk,khd->qhd', weights_low, values_all)
    denominator = lax.optimization_barrier(jnp.sum(weights, -1)).T
    heads_out = (numerator / denominator[:, :, None]).astype(jnp.bfloat16).reshape(FRAMES, head_cols)
    mixed_state = stream + jnp.dot(heads_out, out_weight, preferred_element_type=jnp.float32)
    mlp_in = normed(mixed_state, mlp_gain).astype(jnp.bfloat16)
    hidden_act = jax.nn.gelu(jnp.dot(mlp_in, up_weight, preferred_element_type=jnp.float32)).astype(jnp.bfloat16)
    final_state = mixed_state + jnp.dot(hidden_act, down_weight, preferred_element_type=jnp.float32)
    latents = normed(final_state, final_gain).astype(jnp.bfloat16)

    def readout_block(block_no):
        first_col = (block_no * block_width).astype(jnp.int32)
        rows_part = lax.dynamic_slice_in_dim(readout_weight, first_col, block_width, 0)
        bias_part = lax.dynamic_slice_in_dim(readout_bias, first_col, block_width, 0)
        observed = lax.dynamic_slice_in_dim(spikes, first_col, block_width, 1).astype(jnp.float32)
        log_rate = jnp.dot(latents, rows_part.T, preferred_element_type=jnp.float32) + bias_part[None, :]
        return lax.optimization_barrier(jnp.sum(observed * log_rate - jnp.exp(log_rate), 0))
    model_ll = lax.map(readout_block, jnp.arange(N_NEUR, dtype=jnp.int32)).reshape(NEURONS)
    counts = lax.optimization_barrier(jnp.sum(spikes, 0)).astype(jnp.float32)
    null_ll = counts * jnp.log((counts + 1.0) / FRAMES) - (counts + 1.0)
    heldout = (1 - held_in).astype(jnp.float32)
    gained = heldout * (model_ll - null_ll)
    neuron_bits = gained / (math.log(2.0) * (counts + 1.0))
    bits_per_spike = jnp.sum(gained) / (math.log(2.0) * (1.0 + jnp.sum(heldout * counts)))
    return (latents, neuron_bits, bits_per_spike)
```

```python
import functools
import math

import jax
import jax.numpy as jnp
from jax import lax
from jax.experimental import pallas as pl
from jax.experimental.pallas import tpu as pltpu
from jax.sharding import PartitionSpec as P

HEAD_DIM = 128
OUTER = 4
MESH = pl.DeviceIdType.MESH
BF = jnp.bfloat16
F32 = jnp.float32


def normed(values, gain_vec):
    return values * lax.rsqrt(jnp.mean(values * values, -1, keepdims=True) + 1e-05) * gain_vec


def dot(a, b):
    return jnp.dot(a, b, preferred_element_type=F32)


def dot_nt(a, b):
    return lax.dot_general(a, b, (((1,), (1,)), ((), ())), preferred_element_type=F32)


def kernel(
    n_size,
    t_size,
    spikes_h,
    held_ref,
    readin_h,
    qkv_h,
    out_h,
    up_h,
    down_h,
    ng_ref,
    mg_ref,
    fg_ref,
    readout_h,
    bias_ref,
    lat_out,
    bits_out,
    tot_out,
    spikes_v,
    readin_v,
    qkv_v,
    out_v,
    up_v,
    down_v,
    readout_v,
    load_sems,
    pp,
    core_s,
    core_r,
    s1,
    mid_s,
    mid_r,
    out_s,
    out_r,
    tsum,
    kv,
    lat,
    hid,
    fin,
    core_sems,
    mid_sems,
    outer_sems,
    t_sems,
    kv_sems,
    lat_sems,
    fin_sems,
):
    mid_size = n_size // (2 * OUTER)
    frames, neurons = spikes_v.shape
    rows = frames // n_size
    width = readin_v.shape[1]
    head_cols = out_v.shape[0]
    group = 2 * mid_size * rows
    n = lax.axis_index("neur")
    t = lax.axis_index("tm")
    c = lax.rem(n, 2)
    m = lax.rem(lax.div(n, 2), mid_size)
    o = lax.div(n, 2 * mid_size)

    def nid(oo, mm, cc):
        return (oo * mid_size + mm) * 2 + cc

    def rot(v, d, size):
        return lax.rem(v + d, size)

    def core_peer():
        return (nid(o, m, 1 - c), t)

    def mid_peer(d):
        return (nid(o, rot(m, d, mid_size), c), t)

    def outer_peer(d):
        return (nid(rot(o, d, OUTER), m, c), t)

    def t_peer(d):
        return (n, rot(t, d, t_size))

    loads = []
    for i, (src, dst) in enumerate(
        (
            (spikes_h, spikes_v),
            (readin_h, readin_v),
            (qkv_h, qkv_v),
            (out_h, out_v),
            (up_h, up_v),
            (down_h, down_v),
            (readout_h, readout_v),
        )
    ):
        cp = pltpu.make_async_copy(src, dst, load_sems.at[i])
        cp.start()
        loads.append(cp)

    peers = [core_peer()]
    peers += [mid_peer(d) for d in range(1, mid_size)]
    peers += [outer_peer(d) for d in range(1, OUTER)]
    peers += [t_peer(d) for d in range(1, t_size)]
    barrier = pltpu.get_barrier_semaphore()
    for peer in peers:
        pl.semaphore_signal(barrier, inc=1, device_id=peer, device_id_type=MESH)

    sent = []

    def send(src, dst, sems, index, peer):
        cp = pltpu.make_async_remote_copy(
            src_ref=src,
            dst_ref=dst,
            send_sem=sems.at[(0,) + index],
            recv_sem=sems.at[(1,) + index],
            device_id=peer,
            device_id_type=MESH,
        )
        cp.start()
        sent.append(cp)
        return cp

    def sum_over_t(which, value):
        tsum[which, t] = value.astype(BF)
        cps = [
            send(tsum.at[which, t], tsum.at[which, t], t_sems, (which, d), t_peer(d))
            for d in range(1, t_size)
        ]
        for cp in cps:
            cp.wait_recv()
        total = tsum[which, 0].astype(F32)
        for i in range(1, t_size):
            total = total + tsum[which, i].astype(F32)
        return total

    def gather(buf, sems):
        cps = {}

        def push(do, dm, dc):
            if dc:
                own_m = rot(m, mid_size - dm, mid_size)
                own_o = rot(o, OUTER - do, OUTER)
                peer = core_peer()
            elif dm:
                own_m, own_o = m, rot(o, OUTER - do, OUTER)
                peer = mid_peer(dm)
            else:
                own_m, own_o = m, o
                peer = outer_peer(do)
            block = nid(own_o, own_m, c)
            cps[do, dm, dc] = send(
                buf.at[block], buf.at[block], sems, ((do * mid_size + dm) * 2 + dc,), peer
            )

        for d in range(1, OUTER):
            push(d, 0, 0)
        for d in range(1, mid_size):
            push(0, d, 0)
        push(0, 0, 1)
        for d in range(1, mid_size):
            cps[0, d, 0].wait_recv()
            push(0, d, 1)
        for do in (1, 3, 2):
            cps[do, 0, 0].wait_recv()
            for d in range(1, mid_size):
                push(do, d, 0)
            push(do, 0, 1)
        for do in (1, 3, 2):
            for d in range(1, mid_size):
                cps[do, d, 0].wait_recv()
                push(do, d, 1)
        for do in range(OUTER):
            for d in range(mid_size):
                cps[do, d, 1].wait_recv()

    loads[0].wait()
    loads[1].wait()
    held = held_ref[...]
    order = [2, 1, 3, 0]
    core_cps = {}
    for k, d in enumerate(order):
        at = pl.multiple_of(rot(o, d, OUTER) * group, group)
        masked = (spikes_v[pl.ds(at, group), :] * held).astype(F32).astype(BF)
        pp[d] = dot(masked, readin_v[...]).reshape(mid_size, 2, rows, width)
        for i in range(mid_size):
            core_s[d, i] = pp[d, i, 1 - c].astype(BF)
        if k == 0:
            pl.semaphore_wait(barrier, len(peers))
        core_cps[d] = send(core_s.at[d], core_r.at[d], core_sems, (d,), core_peer())
    mid_cps = {}
    for d in order:
        core_cps[d].wait_recv()
        for dm in list(range(1, mid_size)) + [0]:
            mm = rot(m, dm, mid_size)
            value = pp[d, mm, c] + core_r[d, mm].astype(F32)
            if dm:
                mid_s[d, dm] = value.astype(BF)
                mid_cps[d, dm] = send(
                    mid_s.at[d, dm], mid_r.at[d, dm], mid_sems, (d * mid_size + dm,), mid_peer(dm)
                )
            else:
                s1[d] = value
    outer_cps = {}
    for d in order:
        value = s1[d]
        for dm in range(1, mid_size):
            mid_cps[d, dm].wait_recv()
            value = value + mid_r[d, dm].astype(F32)
        if d:
            out_s[d] = value.astype(BF)
            outer_cps[d] = send(out_s.at[d], out_r.at[d], outer_sems, (d,), outer_peer(d))
    for d in (1, 3, 2):
        outer_cps[d].wait_recv()
        value = value + out_r[d].astype(F32)
    stream = sum_over_t(0, value)

    attn_in = normed(stream, ng_ref[...]).astype(BF)
    loads[2].wait()
    kv[n, :, :head_cols] = dot(attn_in, qkv_v[1]).astype(BF)
    kv[n, :, head_cols:] = dot(attn_in, qkv_v[2]).astype(BF)
    queries = dot(attn_in, qkv_v[0]).astype(BF)
    gather(kv, kv_sems)

    scaling = 1.0 / math.sqrt(HEAD_DIM)
    loads[3].wait()
    heads = []
    for h in range(head_cols // HEAD_DIM):
        cols = slice(h * HEAD_DIM, (h + 1) * HEAD_DIM)
        vcols = slice(head_cols + h * HEAD_DIM, head_cols + (h + 1) * HEAD_DIM)
        keys = kv[:, :, cols].reshape(frames, HEAD_DIM)
        values = kv[:, :, vcols].reshape(frames, HEAD_DIM)
        weights = jnp.exp(dot_nt(queries[:, cols], keys) * scaling)
        denominator = jnp.sum(weights, -1, keepdims=True)
        heads.append((dot(weights.astype(BF), values) / denominator).astype(BF))
    heads_out = heads[0] if len(heads) == 1 else jnp.concatenate(heads, -1)
    mixed_state = stream + sum_over_t(1, dot(heads_out, out_v[...]))

    mlp_in = normed(mixed_state, mg_ref[...]).astype(BF)
    loads[4].wait()
    tile = min(512, up_v.shape[1])
    for i in range(up_v.shape[1] // tile):
        cols = slice(i * tile, (i + 1) * tile)
        hid[:, cols] = jax.nn.gelu(dot(mlp_in, up_v[:, cols])).astype(BF)
    loads[5].wait()
    final_state = mixed_state + sum_over_t(2, dot(hid[...], down_v[...]))
    latents = normed(final_state, fg_ref[...]).astype(BF)
    lat_out[...] = latents
    lat[n] = latents
    gather(lat, lat_sems)

    loads[6].wait()
    blocks = 128 // rows

    def readout_step(i, carry):
        ll, counts = carry
        at = pl.multiple_of(i * blocks * rows, blocks * rows)
        piece = lat[pl.ds(i * blocks, blocks)].reshape(blocks * rows, width)
        log_rate = dot_nt(piece, readout_v[...]) + bias_ref[...]
        observed = spikes_v[pl.ds(at, blocks * rows), :].astype(F32)
        ll = ll + jnp.sum(observed * log_rate - jnp.exp(log_rate), 0, keepdims=True)
        return ll, counts + jnp.sum(observed, 0, keepdims=True)

    zero = jnp.zeros((1, neurons), F32)
    model_ll, counts = lax.fori_loop(0, n_size // blocks, readout_step, (zero, zero))
    heldout = (1 - held).astype(F32)
    null_ll = counts * jnp.log((counts + 1.0) / frames) - (counts + 1.0)
    gained = heldout * (model_ll - null_ll)
    bits_out[...] = gained / (math.log(2.0) * (counts + 1.0))
    score = jnp.sum(gained, -1, keepdims=True)
    spike_sum = jnp.sum(heldout * counts, -1, keepdims=True)
    lane = lax.broadcasted_iota(jnp.int32, (8, 128), 1)
    total = jnp.where(lane == 0, score, jnp.where(lane == 1, spike_sum, 0.0))

    base = 0
    for size, here, peer_of in (
        (2, c, lambda d: core_peer()),
        (mid_size, m, mid_peer),
        (t_size, t, t_peer),
        (OUTER, o, outer_peer),
    ):
        fin[base + here] = total
        cps = [
            send(fin.at[base + here], fin.at[base + here], fin_sems, (base + d,), peer_of(d))
            for d in range(1, size)
        ]
        for cp in cps:
            cp.wait_recv()
        total = fin[base]
        for i in range(1, size):
            total = total + fin[base + i]
        base += size
    score = jnp.sum(jnp.where(lane == 0, total, 0.0), -1, keepdims=True)
    spike_sum = jnp.sum(jnp.where(lane == 1, total, 0.0), -1, keepdims=True)
    tot_out[...] = jnp.broadcast_to(score / (math.log(2.0) * (1.0 + spike_sum)), (8, 128))
    for cp in sent:
        cp.wait_send()


def on_device(
    n_size,
    t_size,
    spikes,
    held_in,
    readin_weight,
    qkv_weight,
    out_weight,
    up_weight,
    down_weight,
    norm_gain,
    mlp_gain,
    final_gain,
    readout_weight,
    readout_bias,
):
    frames, neurons = spikes.shape
    width = readin_weight.shape[1]
    rows = frames // n_size
    mid = n_size // (2 * OUTER)
    head_cols = qkv_weight.shape[2]
    qkv = qkv_weight.transpose(1, 0, 2)
    row = lambda v: v.reshape(1, -1)
    vmem = pl.BlockSpec(memory_space=pltpu.VMEM)
    hbm = pl.BlockSpec(memory_space=pl.ANY)
    dma = pltpu.SemaphoreType.DMA
    n_fin = 2 + mid + t_size + OUTER
    latents, bits, total = pl.pallas_call(
        functools.partial(kernel, n_size, t_size),
        out_shape=(
            jax.ShapeDtypeStruct((rows, width), BF),
            jax.ShapeDtypeStruct((1, neurons), F32),
            jax.ShapeDtypeStruct((8, 128), F32),
        ),
        in_specs=[hbm, vmem, hbm, hbm, hbm, hbm, hbm, vmem, vmem, vmem, hbm, vmem],
        out_specs=(vmem, vmem, vmem),
        scratch_shapes=[
            pltpu.VMEM(spikes.shape, jnp.int32),
            pltpu.VMEM(readin_weight.shape, BF),
            pltpu.VMEM(qkv.shape, BF),
            pltpu.VMEM(out_weight.shape, BF),
            pltpu.VMEM(up_weight.shape, BF),
            pltpu.VMEM(down_weight.shape, BF),
            pltpu.VMEM(readout_weight.shape, BF),
            dma((7,)),
            pltpu.VMEM((OUTER, mid, 2, rows, width), F32),
            pltpu.VMEM((OUTER, mid, rows, width), BF),
            pltpu.VMEM((OUTER, mid, rows, width), BF),
            pltpu.VMEM((OUTER, rows, width), F32),
            pltpu.VMEM((OUTER, mid, rows, width), BF),
            pltpu.VMEM((OUTER, mid, rows, width), BF),
            pltpu.VMEM((OUTER, rows, width), BF),
            pltpu.VMEM((OUTER, rows, width), BF),
            pltpu.VMEM((3, t_size, rows, width), BF),
            pltpu.VMEM((n_size, rows, 2 * head_cols), BF),
            pltpu.VMEM((n_size, rows, width), BF),
            pltpu.VMEM((rows, up_weight.shape[1]), BF),
            pltpu.VMEM((n_fin, 8, 128), F32),
            dma((2, OUTER)),
            dma((2, OUTER * mid)),
            dma((2, OUTER)),
            dma((2, 3, t_size)),
            dma((2, n_size)),
            dma((2, n_size)),
            dma((2, n_fin)),
        ],
        compiler_params=pltpu.CompilerParams(
            collective_id=0, has_side_effects=True, vmem_limit_bytes=52 * 1024 * 1024
        ),
        cost_estimate=pl.CostEstimate(
            flops=4 * frames * neurons * width,
            bytes_accessed=20 * 1024 * 1024,
            transcendentals=frames * neurons,
        ),
    )(
        spikes,
        row(held_in),
        readin_weight,
        qkv,
        out_weight,
        up_weight,
        down_weight,
        row(norm_gain),
        row(mlp_gain),
        row(final_gain),
        readout_weight,
        row(readout_bias),
    )
    return latents, bits.reshape(neurons), total[0, 0]


def solution(mesh):
    in_specs = (
        P(None, ("neur", "tm")),
        P(("neur", "tm")),
        P(("neur", "tm"), None),
        P(None, None, "tm"),
        P("tm", None),
        P(None, "tm"),
        P("tm", None),
        P(),
        P(),
        P(),
        P(("neur", "tm"), None),
        P(("neur", "tm")),
    )
    out_specs = (P("neur", None), P(("neur", "tm")), P())
    return jax.shard_map(
        functools.partial(on_device, mesh.shape["neur"], mesh.shape["tm"]),
        mesh=mesh,
        in_specs=in_specs,
        out_specs=out_specs,
        check_vma=False,
    )
```

```python
import functools
import math

import jax
import jax.numpy as jnp
from jax import lax
from jax.experimental import pallas as pl
from jax.experimental.pallas import tpu as pltpu
from jax.sharding import PartitionSpec as P

HEAD_DIM = 128
OUTER = 4
MESH = pl.DeviceIdType.MESH
BF = jnp.bfloat16
F32 = jnp.float32


def normed(values, gain_vec):
    return values * lax.rsqrt(jnp.mean(values * values, -1, keepdims=True) + 1e-05) * gain_vec


def dot(a, b):
    return jnp.dot(a, b, preferred_element_type=F32)


def dot_nt(a, b):
    return lax.dot_general(a, b, (((1,), (1,)), ((), ())), preferred_element_type=F32)


def kernel(
    n_size,
    t_size,
    spikes_h,
    held_h,
    readin_h,
    qkv_h,
    out_h,
    up_h,
    down_h,
    ng_h,
    mg_h,
    fg_h,
    readout_h,
    bias_h,
    lat_out,
    bits_out,
    tot_out,
    spikes_v,
    readin_v,
    qkv_v,
    out_v,
    up_v,
    down_v,
    readout_v,
    held_ref,
    ng_ref,
    mg_ref,
    fg_ref,
    bias_ref,
    load_sems,
    spike_sems,
    pp,
    core_s,
    core_r,
    s1,
    mid_s,
    mid_r,
    out_s,
    out_r,
    tsum,
    kv,
    lat,
    hid,
    fin,
    core_sems,
    mid_sems,
    outer_sems,
    t_sems,
    kv_sems,
    lat_sems,
    fin_sems,
):
    mid_size = n_size // (2 * OUTER)
    frames, neurons = spikes_v.shape
    rows = frames // n_size
    width = readin_v.shape[1]
    head_cols = out_v.shape[0]
    group = 2 * mid_size * rows
    n = lax.axis_index("neur")
    t = lax.axis_index("tm")
    c = lax.rem(n, 2)
    m = lax.rem(lax.div(n, 2), mid_size)
    o = lax.div(n, 2 * mid_size)

    def nid(oo, mm, cc):
        return (oo * mid_size + mm) * 2 + cc

    def rot(v, d, size):
        return lax.rem(v + d, size)

    def core_peer():
        return (nid(o, m, 1 - c), t)

    def mid_peer(d):
        return (nid(o, rot(m, d, mid_size), c), t)

    def outer_peer(d):
        return (nid(rot(o, d, OUTER), m, c), t)

    def t_peer(d):
        return (n, rot(t, d, t_size))

    loads = []
    for i, (src, dst) in enumerate(
        (
            (held_h, held_ref),
            (readin_h, readin_v),
            (qkv_h, qkv_v),
            (out_h, out_v),
            (up_h, up_v),
            (down_h, down_v),
            (readout_h, readout_v),
            (ng_h, ng_ref),
            (mg_h, mg_ref),
            (fg_h, fg_ref),
            (bias_h, bias_ref),
        )
    ):
        loads.append(pltpu.make_async_copy(src, dst, load_sems.at[i]))
    order = [2, 1, 3, 0]
    starts = {d: pl.multiple_of(rot(o, d, OUTER) * group, group) for d in order}
    spike_loads = {}
    for d in order:
        at = pl.ds(starts[d], group)
        spike_loads[d] = pltpu.make_async_copy(
            spikes_h.at[at, :], spikes_v.at[at, :], spike_sems.at[d]
        )
    loads[0].start()
    spike_loads[order[0]].start()
    loads[1].start()
    for d in order[1:]:
        spike_loads[d].start()

    plane = 2 * mid_size
    line = OUTER * t_size

    def plane_peer(d):
        at = rot(m * 2 + c, d, plane)
        return (o * plane + at, t)

    def line_peer(d):
        at = rot(o * t_size + t, d, line)
        return (nid(lax.div(at, t_size), m, c), lax.rem(at, t_size))

    peers = [plane_peer(d) for d in range(1, plane)]
    peers += [line_peer(d) for d in range(1, line)]
    barrier = pltpu.get_barrier_semaphore()
    for peer in peers:
        pl.semaphore_signal(barrier, inc=1, device_id=peer, device_id_type=MESH)

    sent = []

    def send(src, dst, sems, index, peer):
        cp = pltpu.make_async_remote_copy(
            src_ref=src,
            dst_ref=dst,
            send_sem=sems.at[(0,) + index],
            recv_sem=sems.at[(1,) + index],
            device_id=peer,
            device_id_type=MESH,
        )
        cp.start()
        sent.append(cp)
        return cp

    def sum_over_t(which, pieces):
        wide = width // len(pieces)
        cps = []
        for k, piece in enumerate(pieces):
            cols = slice(k * wide, (k + 1) * wide)
            tsum[which, t, :, cols] = piece().astype(BF)
            for d in range(1, t_size):
                part = tsum.at[which, t, :, cols]
                cps.append(send(part, part, t_sems, (which, k, d), t_peer(d)))
        for cp in cps:
            cp.wait_recv()
        total = tsum[which, 0].astype(F32)
        for i in range(1, t_size):
            total = total + tsum[which, i].astype(F32)
        return total

    def gather(buf, sems, use):
        cps = {}

        def push(do, dm, dc):
            if dc:
                own_m = rot(m, mid_size - dm, mid_size)
                own_o = rot(o, OUTER - do, OUTER)
                peer = core_peer()
            elif dm:
                own_m, own_o = m, rot(o, OUTER - do, OUTER)
                peer = mid_peer(dm)
            else:
                own_m, own_o = m, o
                peer = outer_peer(do)
            block = nid(own_o, own_m, c)
            cps[do, dm, dc] = send(
                buf.at[block], buf.at[block], sems, ((do * mid_size + dm) * 2 + dc,), peer
            )

        def to_mid(do):
            if do:
                cps[do, 0, 0].wait_recv()
            for d in range(1, mid_size):
                push(do, d, 0)
            push(do, 0, 1)

        def to_core(do):
            for d in range(1, mid_size):
                cps[do, d, 0].wait_recv()
                push(do, d, 1)

        def finish(do):
            for d in range(mid_size):
                cps[do, d, 1].wait_recv()
            use(rot(o, OUTER - do, OUTER) * plane)

        for d in (1, 3, 2):
            push(d, 0, 0)
        to_mid(0)
        to_core(0)
        last = 0
        for do in (1, 3, 2):
            to_mid(do)
            finish(last)
            to_core(do)
            last = do
        finish(last)

    core_cps, mid_cps, outer_cps = {}, {}, {}

    def read_in(d):
        spike_loads[d].wait()
        masked = (spikes_v[pl.ds(starts[d], group), :] * held_ref[...]).astype(F32).astype(BF)
        pp[d] = dot(masked, readin_v[...]).reshape(mid_size, 2, rows, width)
        for i in range(mid_size):
            core_s[d, i] = pp[d, i, 1 - c].astype(BF)
        if d == order[0]:
            pl.semaphore_wait(barrier, len(peers))
        core_cps[d] = send(core_s.at[d], core_r.at[d], core_sems, (d,), core_peer())

    def over_mid(d):
        core_cps[d].wait_recv()
        for dm in list(range(1, mid_size)) + [0]:
            mm = rot(m, dm, mid_size)
            value = pp[d, mm, c] + core_r[d, mm].astype(F32)
            if dm:
                mid_s[d, dm] = value.astype(BF)
                mid_cps[d, dm] = send(
                    mid_s.at[d, dm], mid_r.at[d, dm], mid_sems, (d * mid_size + dm,), mid_peer(dm)
                )
            else:
                s1[d] = value

    def over_outer(d):
        value = s1[d]
        for dm in range(1, mid_size):
            mid_cps[d, dm].wait_recv()
            value = value + mid_r[d, dm].astype(F32)
        if d:
            out_s[d] = value.astype(BF)
            outer_cps[d] = send(out_s.at[d], out_r.at[d], outer_sems, (d,), outer_peer(d))
        return value

    loads[0].wait()
    loads[1].wait()
    read_in(2)
    for cp in loads[2:]:
        cp.start()
    read_in(1)
    over_mid(2)
    read_in(3)
    over_mid(1)
    over_outer(2)
    read_in(0)
    over_mid(3)
    over_outer(1)
    over_mid(0)
    over_outer(3)
    value = over_outer(0)
    for d in (2, 1, 3):
        outer_cps[d].wait_recv()
        value = value + out_r[d].astype(F32)
    stream = sum_over_t(0, [lambda: value])

    for cp in loads[7:]:
        cp.wait()
    attn_in = normed(stream, ng_ref[...]).astype(BF)
    loads[2].wait()
    kv[n, :, :head_cols] = dot(attn_in, qkv_v[1]).astype(BF)
    kv[n, :, head_cols:] = dot(attn_in, qkv_v[2]).astype(BF)
    queries = dot(attn_in, qkv_v[0]).astype(BF)

    scaling = 1.0 / math.sqrt(HEAD_DIM)
    local_heads = head_cols // HEAD_DIM
    numer = [jnp.zeros((rows, HEAD_DIM), F32)] * local_heads
    denom = [jnp.zeros((rows, 1), F32)] * local_heads

    def attend(base):
        for h in range(local_heads):
            cols = slice(h * HEAD_DIM, (h + 1) * HEAD_DIM)
            vcols = slice(head_cols + h * HEAD_DIM, head_cols + (h + 1) * HEAD_DIM)
            keys = kv[pl.ds(base, plane), :, cols].reshape(group, HEAD_DIM)
            values = kv[pl.ds(base, plane), :, vcols].reshape(group, HEAD_DIM)
            weights = jnp.exp(dot_nt(queries[:, cols], keys) * scaling)
            denom[h] = denom[h] + jnp.sum(weights, -1, keepdims=True)
            numer[h] = numer[h] + dot(weights.astype(BF), values)

    gather(kv, kv_sems, attend)
    loads[3].wait()
    heads = [(a / b).astype(BF) for a, b in zip(numer, denom)]
    heads_out = heads[0] if len(heads) == 1 else jnp.concatenate(heads, -1)
    half = width // 2
    mixed_state = stream + sum_over_t(
        1,
        [
            lambda: dot(heads_out, out_v[:, :half]),
            lambda: dot(heads_out, out_v[:, half:]),
        ],
    )

    mlp_in = normed(mixed_state, mg_ref[...]).astype(BF)
    loads[4].wait()
    tile = min(512, up_v.shape[1])
    for i in range(up_v.shape[1] // tile):
        cols = slice(i * tile, (i + 1) * tile)
        hid[:, cols] = jax.nn.gelu(dot(mlp_in, up_v[:, cols])).astype(BF)
    loads[5].wait()
    final_state = mixed_state + sum_over_t(
        2,
        [
            lambda: dot(hid[...], down_v[:, :half]),
            lambda: dot(hid[...], down_v[:, half:]),
        ],
    )
    latents = normed(final_state, fg_ref[...]).astype(BF)
    lat_out[...] = latents
    lat[n] = latents
    loads[6].wait()
    sums = [jnp.zeros((1, neurons), F32)] * 2

    def read_out(base):
        piece = lat[pl.ds(base, plane)].reshape(group, width)
        at = pl.multiple_of(base * rows, group)
        log_rate = dot_nt(piece, readout_v[...]) + bias_ref[...]
        observed = spikes_v[pl.ds(at, group), :].astype(F32)
        sums[0] = sums[0] + jnp.sum(observed * log_rate - jnp.exp(log_rate), 0, keepdims=True)
        sums[1] = sums[1] + jnp.sum(observed, 0, keepdims=True)

    gather(lat, lat_sems, read_out)
    model_ll, counts = sums
    held = held_ref[...]
    heldout = (1 - held).astype(F32)
    null_ll = counts * jnp.log((counts + 1.0) / frames) - (counts + 1.0)
    gained = heldout * (model_ll - null_ll)
    bits_out[...] = gained / (math.log(2.0) * (counts + 1.0))
    score = jnp.sum(gained, -1, keepdims=True)
    spike_sum = jnp.sum(heldout * counts, -1, keepdims=True)
    lane = lax.broadcasted_iota(jnp.int32, (8, 128), 1)
    total = jnp.where(lane == 0, score, jnp.where(lane == 1, spike_sum, 0.0))

    base = 0
    for size, here, peer_of in (
        (plane, m * 2 + c, plane_peer),
        (line, o * t_size + t, line_peer),
    ):
        fin[base + here] = total
        cps = [
            send(fin.at[base + here], fin.at[base + here], fin_sems, (base + d,), peer_of(d))
            for d in range(1, size)
        ]
        for cp in cps:
            cp.wait_recv()
        total = fin[base]
        for i in range(1, size):
            total = total + fin[base + i]
        base += size
    score = jnp.sum(jnp.where(lane == 0, total, 0.0), -1, keepdims=True)
    spike_sum = jnp.sum(jnp.where(lane == 1, total, 0.0), -1, keepdims=True)
    tot_out[...] = jnp.broadcast_to(score / (math.log(2.0) * (1.0 + spike_sum)), (8, 128))
    for cp in sent:
        cp.wait_send()


def on_device(
    n_size,
    t_size,
    spikes,
    held_in,
    readin_weight,
    qkv_weight,
    out_weight,
    up_weight,
    down_weight,
    norm_gain,
    mlp_gain,
    final_gain,
    readout_weight,
    readout_bias,
):
    frames, neurons = spikes.shape
    width = readin_weight.shape[1]
    rows = frames // n_size
    mid = n_size // (2 * OUTER)
    head_cols = qkv_weight.shape[2]
    qkv = qkv_weight.transpose(1, 0, 2)
    row = lambda v: v.reshape(1, -1)
    vmem = pl.BlockSpec(memory_space=pltpu.VMEM)
    hbm = pl.BlockSpec(memory_space=pltpu.HBM)
    dma = pltpu.SemaphoreType.DMA
    n_fin = 2 * mid + t_size * OUTER
    latents, bits, total = pl.pallas_call(
        functools.partial(kernel, n_size, t_size),
        out_shape=(
            jax.ShapeDtypeStruct((rows, width), BF),
            jax.ShapeDtypeStruct((1, neurons), F32),
            jax.ShapeDtypeStruct((8, 128), F32),
        ),
        in_specs=[hbm] * 12,
        out_specs=(vmem, vmem, vmem),
        scratch_shapes=[
            pltpu.VMEM(spikes.shape, jnp.int32),
            pltpu.VMEM(readin_weight.shape, BF),
            pltpu.VMEM(qkv.shape, BF),
            pltpu.VMEM(out_weight.shape, BF),
            pltpu.VMEM(up_weight.shape, BF),
            pltpu.VMEM(down_weight.shape, BF),
            pltpu.VMEM(readout_weight.shape, BF),
            pltpu.VMEM((1, neurons), jnp.int32),
            pltpu.VMEM((1, width), F32),
            pltpu.VMEM((1, width), F32),
            pltpu.VMEM((1, width), F32),
            pltpu.VMEM((1, neurons), F32),
            dma((11,)),
            dma((OUTER,)),
            pltpu.VMEM((OUTER, mid, 2, rows, width), F32),
            pltpu.VMEM((OUTER, mid, rows, width), BF),
            pltpu.VMEM((OUTER, mid, rows, width), BF),
            pltpu.VMEM((OUTER, rows, width), F32),
            pltpu.VMEM((OUTER, mid, rows, width), BF),
            pltpu.VMEM((OUTER, mid, rows, width), BF),
            pltpu.VMEM((OUTER, rows, width), BF),
            pltpu.VMEM((OUTER, rows, width), BF),
            pltpu.VMEM((3, t_size, rows, width), BF),
            pltpu.VMEM((n_size, rows, 2 * head_cols), BF),
            pltpu.VMEM((n_size, rows, width), BF),
            pltpu.VMEM((rows, up_weight.shape[1]), BF),
            pltpu.VMEM((n_fin, 8, 128), F32),
            dma((2, OUTER)),
            dma((2, OUTER * mid)),
            dma((2, OUTER)),
            dma((2, 3, 2, t_size)),
            dma((2, n_size)),
            dma((2, n_size)),
            dma((2, n_fin)),
        ],
        compiler_params=pltpu.CompilerParams(
            collective_id=0, has_side_effects=True, vmem_limit_bytes=60 * 1024 * 1024
        ),
        cost_estimate=pl.CostEstimate(
            flops=4 * frames * neurons * width,
            bytes_accessed=20 * 1024 * 1024,
            transcendentals=frames * neurons,
        ),
    )(
        spikes,
        row(held_in),
        readin_weight,
        qkv,
        out_weight,
        up_weight,
        down_weight,
        row(norm_gain),
        row(mlp_gain),
        row(final_gain),
        readout_weight,
        row(readout_bias),
    )
    return latents, bits.reshape(neurons), total[0, 0]


def solution(mesh):
    in_specs = (
        P(None, ("neur", "tm")),
        P(("neur", "tm")),
        P(("neur", "tm"), None),
        P(None, None, "tm"),
        P("tm", None),
        P(None, "tm"),
        P("tm", None),
        P(),
        P(),
        P(),
        P(("neur", "tm"), None),
        P(("neur", "tm")),
    )
    out_specs = (P("neur", None), P(("neur", "tm")), P())
    return jax.shard_map(
        functools.partial(on_device, mesh.shape["neur"], mesh.shape["tm"]),
        mesh=mesh,
        in_specs=in_specs,
        out_specs=out_specs,
        check_vma=False,
    )
```

```python
import functools
import math

import jax
import jax.numpy as jnp
from jax import lax
from jax.experimental import pallas as pl
from jax.experimental.pallas import tpu as pltpu
from jax.sharding import PartitionSpec as P

HEAD_DIM = 128
OUTER = 4
MESH = pl.DeviceIdType.MESH
BF = jnp.bfloat16
F32 = jnp.float32


def normed(values, gain_vec):
    return values * lax.rsqrt(jnp.mean(values * values, -1, keepdims=True) + 1e-05) * gain_vec


def dot(a, b):
    return jnp.dot(a, b, preferred_element_type=F32)


def dot_nt(a, b):
    return lax.dot_general(a, b, (((1,), (1,)), ((), ())), preferred_element_type=F32)


def kernel(
    n_size,
    t_size,
    spikes_h,
    held_h,
    readin_h,
    qkv_h,
    out_h,
    up_h,
    down_h,
    ng_h,
    mg_h,
    fg_h,
    readout_h,
    bias_h,
    lat_out,
    bits_out,
    tot_out,
    spikes_v,
    readin_v,
    qkv_v,
    out_v,
    up_v,
    down_v,
    readout_v,
    held_ref,
    ng_ref,
    mg_ref,
    fg_ref,
    bias_ref,
    load_sems,
    spike_sems,
    pp,
    core_s,
    core_r,
    s1,
    mid_s,
    mid_r,
    out_s,
    out_r,
    tsum,
    kv,
    pieces,
    done_s,
    done_r,
    lat,
    hid,
    fin,
    core_sems,
    mid_sems,
    outer_sems,
    t_sems,
    kv_sems,
    lat_sems,
    fin_sems,
):
    mid_size = n_size // (2 * OUTER)
    frames, neurons = spikes_v.shape
    rows = frames // n_size
    width = readin_v.shape[1]
    head_cols = out_v.shape[0]
    group = 2 * mid_size * rows
    n = lax.axis_index("neur")
    t = lax.axis_index("tm")
    c = lax.rem(n, 2)
    m = lax.rem(lax.div(n, 2), mid_size)
    o = lax.div(n, 2 * mid_size)

    def nid(oo, mm, cc):
        return (oo * mid_size + mm) * 2 + cc

    def rot(v, d, size):
        return lax.rem(v + d, size)

    def core_peer():
        return (nid(o, m, 1 - c), t)

    def mid_peer(d):
        return (nid(o, rot(m, d, mid_size), c), t)

    def outer_peer(d):
        return (nid(rot(o, d, OUTER), m, c), t)

    def t_peer(d):
        return (n, rot(t, d, t_size))

    loads = []
    for i, (src, dst) in enumerate(
        (
            (held_h, held_ref),
            (readin_h, readin_v),
            (qkv_h, qkv_v),
            (out_h, out_v),
            (up_h, up_v),
            (down_h, down_v),
            (readout_h, readout_v),
            (ng_h, ng_ref),
            (mg_h, mg_ref),
            (fg_h, fg_ref),
            (bias_h, bias_ref),
        )
    ):
        loads.append(pltpu.make_async_copy(src, dst, load_sems.at[i]))
    order = [2, 1, 3, 0]
    starts = {d: pl.multiple_of(rot(o, d, OUTER) * group, group) for d in order}
    spike_loads = {}
    for d in order:
        at = pl.ds(starts[d], group)
        spike_loads[d] = pltpu.make_async_copy(
            spikes_h.at[at, :], spikes_v.at[at, :], spike_sems.at[d]
        )
    loads[0].start()
    spike_loads[order[0]].start()
    loads[1].start()
    for d in order[1:]:
        spike_loads[d].start()

    plane = 2 * mid_size
    line = OUTER * t_size

    def plane_peer(d):
        at = rot(m * 2 + c, d, plane)
        return (o * plane + at, t)

    def line_peer(d):
        at = rot(o * t_size + t, d, line)
        return (nid(lax.div(at, t_size), m, c), lax.rem(at, t_size))

    peers = [plane_peer(d) for d in range(1, plane)]
    peers += [line_peer(d) for d in range(1, line)]
    barrier = pltpu.get_barrier_semaphore()
    for peer in peers:
        pl.semaphore_signal(barrier, inc=1, device_id=peer, device_id_type=MESH)

    sent = []

    def send(src, dst, sems, index, peer):
        cp = pltpu.make_async_remote_copy(
            src_ref=src,
            dst_ref=dst,
            send_sem=sems.at[(0,) + index],
            recv_sem=sems.at[(1,) + index],
            device_id=peer,
            device_id_type=MESH,
        )
        cp.start()
        sent.append(cp)
        return cp

    def sum_over_t(which, pieces):
        wide = width // len(pieces)
        cps = []
        for k, piece in enumerate(pieces):
            cols = slice(k * wide, (k + 1) * wide)
            tsum[which, t, :, cols] = piece().astype(BF)
            for d in range(1, t_size):
                part = tsum.at[which, t, :, cols]
                cps.append(send(part, part, t_sems, (which, k, d), t_peer(d)))
        for cp in cps:
            cp.wait_recv()
        total = tsum[which, 0].astype(F32)
        for i in range(1, t_size):
            total = total + tsum[which, i].astype(F32)
        return total

    def gather(buf, sems, use):
        cps = {}

        def push(do, dm, dc):
            if dc:
                own_m = rot(m, mid_size - dm, mid_size)
                own_o = rot(o, OUTER - do, OUTER)
                peer = core_peer()
            elif dm:
                own_m, own_o = m, rot(o, OUTER - do, OUTER)
                peer = mid_peer(dm)
            else:
                own_m, own_o = m, o
                peer = outer_peer(do)
            block = nid(own_o, own_m, c)
            cps[do, dm, dc] = send(
                buf.at[block], buf.at[block], sems, ((do * mid_size + dm) * 2 + dc,), peer
            )

        def to_mid(do):
            if do:
                cps[do, 0, 0].wait_recv()
            for d in range(1, mid_size):
                push(do, d, 0)
            push(do, 0, 1)

        def to_core(do):
            for d in range(1, mid_size):
                cps[do, d, 0].wait_recv()
                push(do, d, 1)

        def finish(do):
            for d in range(mid_size):
                cps[do, d, 1].wait_recv()
            use(rot(o, OUTER - do, OUTER) * plane)

        push(1, 0, 0)
        push(3, 0, 0)
        to_mid(0)
        to_core(0)
        for d in (1, 3):
            cps[d, 0, 0].wait_send()
            sent[:] = [cp for cp in sent if cp is not cps[d, 0, 0]]
        push(2, 0, 0)
        to_mid(1)
        to_mid(3)
        finish(0)
        to_core(1)
        to_core(3)
        to_mid(2)
        finish(1)
        to_core(2)
        finish(3)
        finish(2)

    core_cps, mid_cps, outer_cps = {}, {}, {}

    def read_in(d):
        spike_loads[d].wait()
        masked = (spikes_v[pl.ds(starts[d], group), :] * held_ref[...]).astype(F32).astype(BF)
        pp[d] = dot(masked, readin_v[...]).reshape(mid_size, 2, rows, width)
        for i in range(mid_size):
            core_s[d, i] = pp[d, i, 1 - c].astype(BF)
        if d == order[0]:
            pl.semaphore_wait(barrier, len(peers))
        core_cps[d] = send(core_s.at[d], core_r.at[d], core_sems, (d,), core_peer())

    def over_mid(d):
        core_cps[d].wait_recv()
        for dm in list(range(1, mid_size)) + [0]:
            mm = rot(m, dm, mid_size)
            value = pp[d, mm, c] + core_r[d, mm].astype(F32)
            if dm:
                mid_s[d, dm] = value.astype(BF)
                mid_cps[d, dm] = send(
                    mid_s.at[d, dm], mid_r.at[d, dm], mid_sems, (d * mid_size + dm,), mid_peer(dm)
                )
            else:
                s1[d] = value

    def over_outer(d):
        value = s1[d]
        for dm in range(1, mid_size):
            mid_cps[d, dm].wait_recv()
            value = value + mid_r[d, dm].astype(F32)
        if d:
            out_s[d] = value.astype(BF)
            outer_cps[d] = send(out_s.at[d], out_r.at[d], outer_sems, (d,), outer_peer(d))
        return value

    loads[0].wait()
    loads[1].wait()
    read_in(2)
    for cp in loads[2:]:
        cp.start()
    read_in(1)
    over_mid(2)
    read_in(3)
    over_mid(1)
    over_outer(2)
    read_in(0)
    over_mid(3)
    over_outer(1)
    over_mid(0)
    over_outer(3)
    value = over_outer(0)
    for d in (2, 1, 3):
        outer_cps[d].wait_recv()
        value = value + out_r[d].astype(F32)
    stream = sum_over_t(0, [lambda: value])

    for cp in loads[7:]:
        cp.wait()
    attn_in = normed(stream, ng_ref[...]).astype(BF)
    loads[2].wait()
    projected = [dot(attn_in, qkv_v[i]).astype(BF) for i in range(3)]
    loads[3].wait()
    scaling = 1.0 / math.sqrt(HEAD_DIM)
    local_heads = head_cols // HEAD_DIM
    head_at = [slice(h * HEAD_DIM, (h + 1) * HEAD_DIM) for h in range(local_heads)]

    def attend(query, keys, values, sums):
        weights = jnp.exp(dot_nt(query, keys) * scaling)
        return (
            sums[0] + dot(weights.astype(BF), values),
            sums[1] + jnp.sum(weights, -1, keepdims=True),
        )

    if local_heads == OUTER:
        spot = m * 2 + c
        for h in range(OUTER):
            for i in range(3):
                pieces[h, :, head_at[i]] = projected[i][:, head_at[h]]
        turned = [
            send(
                pieces.at[rot(o, d, OUTER)], kv.at[spot, o], kv_sems, (d,), outer_peer(d)
            )
            for d in (2, 1, 3)
        ]
        kv[spot, o] = pieces[o]
        for cp in turned:
            cp.wait_recv()
        spread = []
        for d in range(1, plane):
            part = kv.at[spot, :, :, HEAD_DIM : 3 * HEAD_DIM]
            spread.append(send(part, part, kv_sems, (OUTER + d,), plane_peer(d)))
        query = kv[spot, :, :, head_at[0]].reshape(OUTER * rows, HEAD_DIM)
        sums = (jnp.zeros(query.shape, F32), jnp.zeros((OUTER * rows, 1), F32))
        for d in range(plane):
            if d:
                spread[d - 1].wait_recv()
            there = rot(spot, plane - d, plane)
            keys = kv[there, :, :, head_at[1]].reshape(OUTER * rows, HEAD_DIM)
            values = kv[there, :, :, head_at[2]].reshape(OUTER * rows, HEAD_DIM)
            sums = attend(query, keys, values, sums)
        done_s[...] = (sums[0] / sums[1]).astype(BF).reshape(OUTER, rows, HEAD_DIM)
        back = [
            send(
                done_s.at[rot(o, d, OUTER)],
                done_r.at[o],
                kv_sems,
                (OUTER + plane + d,),
                outer_peer(d),
            )
            for d in (2, 1, 3)
        ]
        done_r[o] = done_s[o]
        for cp in back:
            cp.wait_recv()
        heads = [done_r[h] for h in range(OUTER)]
    else:
        kv[n, :, :head_cols] = projected[1]
        kv[n, :, head_cols:] = projected[2]
        sums = [(jnp.zeros((rows, HEAD_DIM), F32), jnp.zeros((rows, 1), F32))] * local_heads

        def attend_group(base):
            for h in range(local_heads):
                vcols = slice(head_cols + h * HEAD_DIM, head_cols + (h + 1) * HEAD_DIM)
                keys = kv[pl.ds(base, plane), :, head_at[h]].reshape(group, HEAD_DIM)
                values = kv[pl.ds(base, plane), :, vcols].reshape(group, HEAD_DIM)
                sums[h] = attend(projected[0][:, head_at[h]], keys, values, sums[h])

        gather(kv, kv_sems, attend_group)
        heads = [(a / b).astype(BF) for a, b in sums]
    heads_out = heads[0] if len(heads) == 1 else jnp.concatenate(heads, -1)
    half = width // 2
    mixed_state = stream + sum_over_t(
        1,
        [
            lambda: dot(heads_out, out_v[:, :half]),
            lambda: dot(heads_out, out_v[:, half:]),
        ],
    )

    mlp_in = normed(mixed_state, mg_ref[...]).astype(BF)
    loads[4].wait()
    tile = min(512, up_v.shape[1])
    for i in range(up_v.shape[1] // tile):
        cols = slice(i * tile, (i + 1) * tile)
        hid[:, cols] = jax.nn.gelu(dot(mlp_in, up_v[:, cols])).astype(BF)
    loads[5].wait()
    final_state = mixed_state + sum_over_t(
        2,
        [
            lambda: dot(hid[...], down_v[:, :half]),
            lambda: dot(hid[...], down_v[:, half:]),
        ],
    )
    latents = normed(final_state, fg_ref[...]).astype(BF)
    lat_out[...] = latents
    lat[n] = latents
    loads[6].wait()
    sums = [jnp.zeros((1, neurons), F32)] * 2

    def read_out(base):
        piece = lat[pl.ds(base, plane)].reshape(group, width)
        at = pl.multiple_of(base * rows, group)
        log_rate = dot_nt(piece, readout_v[...]) + bias_ref[...]
        observed = spikes_v[pl.ds(at, group), :].astype(F32)
        sums[0] = sums[0] + jnp.sum(observed * log_rate - jnp.exp(log_rate), 0, keepdims=True)
        sums[1] = sums[1] + jnp.sum(observed, 0, keepdims=True)

    gather(lat, lat_sems, read_out)
    model_ll, counts = sums
    held = held_ref[...]
    heldout = (1 - held).astype(F32)
    null_ll = counts * jnp.log((counts + 1.0) / frames) - (counts + 1.0)
    gained = heldout * (model_ll - null_ll)
    bits_out[...] = gained / (math.log(2.0) * (counts + 1.0))
    score = jnp.sum(gained, -1, keepdims=True)
    spike_sum = jnp.sum(heldout * counts, -1, keepdims=True)
    lane = lax.broadcasted_iota(jnp.int32, (8, 128), 1)
    total = jnp.where(lane == 0, score, jnp.where(lane == 1, spike_sum, 0.0))

    base = 0
    for size, here, peer_of in (
        (plane, m * 2 + c, plane_peer),
        (line, o * t_size + t, line_peer),
    ):
        fin[base + here] = total
        cps = [
            send(fin.at[base + here], fin.at[base + here], fin_sems, (base + d,), peer_of(d))
            for d in range(1, size)
        ]
        for cp in cps:
            cp.wait_recv()
        total = fin[base]
        for i in range(1, size):
            total = total + fin[base + i]
        base += size
    score = jnp.sum(jnp.where(lane == 0, total, 0.0), -1, keepdims=True)
    spike_sum = jnp.sum(jnp.where(lane == 1, total, 0.0), -1, keepdims=True)
    tot_out[...] = jnp.broadcast_to(score / (math.log(2.0) * (1.0 + spike_sum)), (8, 128))
    for cp in sent:
        cp.wait_send()


def on_device(
    n_size,
    t_size,
    spikes,
    held_in,
    readin_weight,
    qkv_weight,
    out_weight,
    up_weight,
    down_weight,
    norm_gain,
    mlp_gain,
    final_gain,
    readout_weight,
    readout_bias,
):
    frames, neurons = spikes.shape
    width = readin_weight.shape[1]
    rows = frames // n_size
    mid = n_size // (2 * OUTER)
    head_cols = qkv_weight.shape[2]
    qkv = qkv_weight.transpose(1, 0, 2)
    row = lambda v: v.reshape(1, -1)
    vmem = pl.BlockSpec(memory_space=pltpu.VMEM)
    hbm = pl.BlockSpec(memory_space=pltpu.HBM)
    dma = pltpu.SemaphoreType.DMA
    by_head = head_cols == OUTER * HEAD_DIM
    kv_shape = (
        (2 * mid, OUTER, rows, 3 * HEAD_DIM) if by_head else (n_size, rows, 2 * head_cols)
    )
    n_kv = 2 * OUTER + 2 * mid if by_head else n_size
    n_fin = 2 * mid + t_size * OUTER
    latents, bits, total = pl.pallas_call(
        functools.partial(kernel, n_size, t_size),
        out_shape=(
            jax.ShapeDtypeStruct((rows, width), BF),
            jax.ShapeDtypeStruct((1, neurons), F32),
            jax.ShapeDtypeStruct((8, 128), F32),
        ),
        in_specs=[hbm] * 12,
        out_specs=(vmem, vmem, vmem),
        scratch_shapes=[
            pltpu.VMEM(spikes.shape, jnp.int32),
            pltpu.VMEM(readin_weight.shape, BF),
            pltpu.VMEM(qkv.shape, BF),
            pltpu.VMEM(out_weight.shape, BF),
            pltpu.VMEM(up_weight.shape, BF),
            pltpu.VMEM(down_weight.shape, BF),
            pltpu.VMEM(readout_weight.shape, BF),
            pltpu.VMEM((1, neurons), jnp.int32),
            pltpu.VMEM((1, width), F32),
            pltpu.VMEM((1, width), F32),
            pltpu.VMEM((1, width), F32),
            pltpu.VMEM((1, neurons), F32),
            dma((11,)),
            dma((OUTER,)),
            pltpu.VMEM((OUTER, mid, 2, rows, width), F32),
            pltpu.VMEM((OUTER, mid, rows, width), BF),
            pltpu.VMEM((OUTER, mid, rows, width), BF),
            pltpu.VMEM((OUTER, rows, width), F32),
            pltpu.VMEM((OUTER, mid, rows, width), BF),
            pltpu.VMEM((OUTER, mid, rows, width), BF),
            pltpu.VMEM((OUTER, rows, width), BF),
            pltpu.VMEM((OUTER, rows, width), BF),
            pltpu.VMEM((3, t_size, rows, width), BF),
            pltpu.VMEM(kv_shape, BF),
            pltpu.VMEM((OUTER, rows, 3 * HEAD_DIM), BF),
            pltpu.VMEM((OUTER, rows, HEAD_DIM), BF),
            pltpu.VMEM((OUTER, rows, HEAD_DIM), BF),
            pltpu.VMEM((n_size, rows, width), BF),
            pltpu.VMEM((rows, up_weight.shape[1]), BF),
            pltpu.VMEM((n_fin, 8, 128), F32),
            dma((2, OUTER)),
            dma((2, OUTER * mid)),
            dma((2, OUTER)),
            dma((2, 3, 2, t_size)),
            dma((2, n_kv)),
            dma((2, n_size)),
            dma((2, n_fin)),
        ],
        compiler_params=pltpu.CompilerParams(
            collective_id=0, has_side_effects=True, vmem_limit_bytes=40 * 1024 * 1024
        ),
        cost_estimate=pl.CostEstimate(
            flops=4 * frames * neurons * width,
            bytes_accessed=20 * 1024 * 1024,
            transcendentals=frames * neurons,
        ),
    )(
        spikes,
        row(held_in),
        readin_weight,
        qkv,
        out_weight,
        up_weight,
        down_weight,
        row(norm_gain),
        row(mlp_gain),
        row(final_gain),
        readout_weight,
        row(readout_bias),
    )
    return latents, bits.reshape(neurons), total[0, 0]


def solution(mesh):
    in_specs = (
        P(None, ("neur", "tm")),
        P(("neur", "tm")),
        P(("neur", "tm"), None),
        P(None, None, "tm"),
        P("tm", None),
        P(None, "tm"),
        P("tm", None),
        P(),
        P(),
        P(),
        P(("neur", "tm"), None),
        P(("neur", "tm")),
    )
    out_specs = (P("neur", None), P(("neur", "tm")), P())
    return jax.shard_map(
        functools.partial(on_device, mesh.shape["neur"], mesh.shape["tm"]),
        mesh=mesh,
        in_specs=in_specs,
        out_specs=out_specs,
        check_vma=False,
    )
```

```python
import functools
import math

import jax
import jax.numpy as jnp
from jax import lax
from jax.experimental import pallas as pl
from jax.experimental.pallas import tpu as pltpu
from jax.sharding import PartitionSpec as P

HEAD_DIM = 128
OUTER = 4
MESH = pl.DeviceIdType.MESH
BF = jnp.bfloat16
F32 = jnp.float32


def normed(values, gain_vec):
    return values * lax.rsqrt(jnp.mean(values * values, -1, keepdims=True) + 1e-05) * gain_vec


def dot(a, b):
    return jnp.dot(a, b, preferred_element_type=F32)


def dot_nt(a, b):
    return lax.dot_general(a, b, (((1,), (1,)), ((), ())), preferred_element_type=F32)


def kernel(
    n_size,
    t_size,
    spikes_h,
    held_h,
    readin_h,
    qkv_h,
    out_h,
    up_h,
    down_h,
    ng_h,
    mg_h,
    fg_h,
    readout_h,
    bias_h,
    lat_out,
    bits_out,
    tot_out,
    spikes_v,
    readin_v,
    qkv_v,
    out_v,
    up_v,
    down_v,
    readout_v,
    held_ref,
    ng_ref,
    mg_ref,
    fg_ref,
    bias_ref,
    load_sems,
    spike_sems,
    pp,
    core_s,
    core_r,
    s1,
    mid_s,
    mid_r,
    out_s,
    out_r,
    tsum,
    kv,
    pieces,
    done_s,
    done_r,
    lat,
    hid,
    fin,
    core_sems,
    mid_sems,
    outer_sems,
    t_sems,
    kv_sems,
    lat_sems,
    fin_sems,
):
    mid_size = n_size // (2 * OUTER)
    frames, neurons = spikes_v.shape
    rows = frames // n_size
    width = readin_v.shape[1]
    head_cols = out_v.shape[0]
    group = 2 * mid_size * rows
    n = lax.axis_index("neur")
    t = lax.axis_index("tm")
    c = lax.rem(n, 2)
    m = lax.rem(lax.div(n, 2), mid_size)
    o = lax.div(n, 2 * mid_size)

    def nid(oo, mm, cc):
        return (oo * mid_size + mm) * 2 + cc

    def rot(v, d, size):
        return lax.rem(v + d, size)

    def core_peer():
        return (nid(o, m, 1 - c), t)

    def mid_peer(d):
        return (nid(o, rot(m, d, mid_size), c), t)

    def outer_peer(d):
        return (nid(rot(o, d, OUTER), m, c), t)

    def t_peer(d):
        return (n, rot(t, d, t_size))

    loads = []
    for i, (src, dst) in enumerate(
        (
            (held_h, held_ref),
            (qkv_h, qkv_v),
            (out_h, out_v),
            (up_h, up_v),
            (down_h, down_v),
            (readout_h, readout_v),
            (ng_h, ng_ref),
            (mg_h, mg_ref),
            (fg_h, fg_ref),
            (bias_h, bias_ref),
        )
    ):
        loads.append(pltpu.make_async_copy(src, dst, load_sems.at[i]))
    order = [2, 1, 3, 0]
    starts = {d: pl.multiple_of(rot(o, d, OUTER) * group, group) for d in order}
    spike_loads = {}
    for d in order:
        at = pl.ds(starts[d], group)
        spike_loads[d] = pltpu.make_async_copy(
            spikes_h.at[at, :], spikes_v.at[at, :], spike_sems.at[d]
        )
    quarter = readin_v.shape[0] // 4
    readin_loads = []
    for i in range(4):
        at = pl.ds(i * quarter, quarter)
        readin_loads.append(
            pltpu.make_async_copy(readin_h.at[at, :], readin_v.at[at, :], spike_sems.at[OUTER + i])
        )
    loads[0].start()
    spike_loads[order[0]].start()
    for cp in readin_loads:
        cp.start()
    for d in order[1:]:
        spike_loads[d].start()

    plane = 2 * mid_size
    line = OUTER * t_size

    def plane_peer(d):
        at = rot(m * 2 + c, d, plane)
        return (o * plane + at, t)

    def line_peer(d):
        at = rot(o * t_size + t, d, line)
        return (nid(lax.div(at, t_size), m, c), lax.rem(at, t_size))

    peers = [plane_peer(d) for d in range(1, plane)]
    peers += [line_peer(d) for d in range(1, line)]
    barrier = pltpu.get_barrier_semaphore()
    for peer in peers:
        pl.semaphore_signal(barrier, inc=1, device_id=peer, device_id_type=MESH)

    sent = []

    def send(src, dst, sems, index, peer):
        cp = pltpu.make_async_remote_copy(
            src_ref=src,
            dst_ref=dst,
            send_sem=sems.at[(0,) + index],
            recv_sem=sems.at[(1,) + index],
            device_id=peer,
            device_id_type=MESH,
        )
        cp.start()
        sent.append(cp)
        return cp

    def sum_over_t(which, pieces):
        wide = width // len(pieces)
        cps = []
        for k, piece in enumerate(pieces):
            cols = slice(k * wide, (k + 1) * wide)
            tsum[which, t, :, cols] = piece().astype(BF)
            for d in range(1, t_size):
                part = tsum.at[which, t, :, cols]
                cps.append(send(part, part, t_sems, (which, k, d), t_peer(d)))
        for cp in cps:
            cp.wait_recv()
        total = tsum[which, 0].astype(F32)
        for i in range(1, t_size):
            total = total + tsum[which, i].astype(F32)
        return total

    def gather(buf, sems, use):
        cps = {}

        def push(do, dm, dc):
            if dc:
                own_m = rot(m, mid_size - dm, mid_size)
                own_o = rot(o, OUTER - do, OUTER)
                peer = core_peer()
            elif dm:
                own_m, own_o = m, rot(o, OUTER - do, OUTER)
                peer = mid_peer(dm)
            else:
                own_m, own_o = m, o
                peer = outer_peer(do)
            block = nid(own_o, own_m, c)
            cps[do, dm, dc] = send(
                buf.at[block], buf.at[block], sems, ((do * mid_size + dm) * 2 + dc,), peer
            )

        def to_mid(do):
            if do:
                cps[do, 0, 0].wait_recv()
            for d in range(1, mid_size):
                push(do, d, 0)
            push(do, 0, 1)

        def to_core(do):
            for d in range(1, mid_size):
                cps[do, d, 0].wait_recv()
                push(do, d, 1)

        def finish(do):
            for d in range(mid_size):
                cps[do, d, 1].wait_recv()
            use(rot(o, OUTER - do, OUTER) * plane)

        push(1, 0, 0)
        push(3, 0, 0)
        to_mid(0)
        to_core(0)
        for d in (1, 3):
            cps[d, 0, 0].wait_send()
            sent[:] = [cp for cp in sent if cp is not cps[d, 0, 0]]
        push(2, 0, 0)
        to_mid(1)
        to_mid(3)
        finish(0)
        to_core(1)
        to_core(3)
        to_mid(2)
        finish(1)
        to_core(2)
        finish(3)
        finish(2)

    core_cps, mid_cps, outer_cps = {}, {}, {}

    def read_in(d):
        spike_loads[d].wait()
        masked = (spikes_v[pl.ds(starts[d], group), :] * held_ref[...]).astype(F32).astype(BF)
        pp[d] = dot(masked, readin_v[...]).reshape(mid_size, 2, rows, width)
        for i in range(mid_size):
            core_s[d, i] = pp[d, i, 1 - c].astype(BF)
        if d == order[0]:
            pl.semaphore_wait(barrier, len(peers))
        core_cps[d] = send(core_s.at[d], core_r.at[d], core_sems, (d,), core_peer())

    def over_mid(d):
        core_cps[d].wait_recv()
        for dm in list(range(1, mid_size)) + [0]:
            mm = rot(m, dm, mid_size)
            value = pp[d, mm, c] + core_r[d, mm].astype(F32)
            if dm:
                mid_s[d, dm] = value.astype(BF)
                mid_cps[d, dm] = send(
                    mid_s.at[d, dm], mid_r.at[d, dm], mid_sems, (d * mid_size + dm,), mid_peer(dm)
                )
            else:
                s1[d] = value

    def over_outer(d):
        value = s1[d]
        for dm in range(1, mid_size):
            mid_cps[d, dm].wait_recv()
            value = value + mid_r[d, dm].astype(F32)
        if d:
            out_s[d] = value.astype(BF)
            outer_cps[d] = send(out_s.at[d], out_r.at[d], outer_sems, (d,), outer_peer(d))
        return value

    loads[0].wait()
    for cp in readin_loads:
        cp.wait()
    read_in(2)
    for cp in loads[1:]:
        cp.start()
    read_in(1)
    over_mid(2)
    read_in(3)
    over_mid(1)
    over_outer(2)
    read_in(0)
    over_mid(3)
    over_outer(1)
    over_mid(0)
    over_outer(3)
    value = over_outer(0)
    for d in (2, 1, 3):
        outer_cps[d].wait_recv()
        value = value + out_r[d].astype(F32)
    stream = sum_over_t(0, [lambda: value])

    for cp in loads[6:]:
        cp.wait()
    attn_in = normed(stream, ng_ref[...]).astype(BF)
    loads[1].wait()
    projected = [dot(attn_in, qkv_v[i]).astype(BF) for i in range(3)]
    loads[2].wait()
    scaling = 1.0 / math.sqrt(HEAD_DIM)
    local_heads = head_cols // HEAD_DIM
    head_at = [slice(h * HEAD_DIM, (h + 1) * HEAD_DIM) for h in range(local_heads)]

    def attend(query, keys, values, sums):
        weights = jnp.exp(dot_nt(query, keys) * scaling)
        return (
            sums[0] + dot(weights.astype(BF), values),
            sums[1] + jnp.sum(weights, -1, keepdims=True),
        )

    if local_heads == OUTER:
        spot = m * 2 + c
        for h in range(OUTER):
            for i in range(3):
                pieces[h, :, head_at[i]] = projected[i][:, head_at[h]]
        turned = [
            send(
                pieces.at[rot(o, d, OUTER)], kv.at[spot, o], kv_sems, (d,), outer_peer(d)
            )
            for d in (2, 1, 3)
        ]
        kv[spot, o] = pieces[o]
        for cp in turned:
            cp.wait_recv()
        spread = []
        for d in range(1, plane):
            part = kv.at[spot, :, :, HEAD_DIM : 3 * HEAD_DIM]
            spread.append(send(part, part, kv_sems, (OUTER + d,), plane_peer(d)))
        query = kv[spot, :, :, head_at[0]].reshape(OUTER * rows, HEAD_DIM)
        sums = (jnp.zeros(query.shape, F32), jnp.zeros((OUTER * rows, 1), F32))
        for d in range(plane):
            if d:
                spread[d - 1].wait_recv()
            there = rot(spot, plane - d, plane)
            keys = kv[there, :, :, head_at[1]].reshape(OUTER * rows, HEAD_DIM)
            values = kv[there, :, :, head_at[2]].reshape(OUTER * rows, HEAD_DIM)
            sums = attend(query, keys, values, sums)
        done_s[...] = (sums[0] / sums[1]).astype(BF).reshape(OUTER, rows, HEAD_DIM)
        back = [
            send(
                done_s.at[rot(o, d, OUTER)],
                done_r.at[o],
                kv_sems,
                (OUTER + plane + d,),
                outer_peer(d),
            )
            for d in (2, 1, 3)
        ]
        done_r[o] = done_s[o]
        for cp in back:
            cp.wait_recv()
        heads = [done_r[h] for h in range(OUTER)]
    else:
        kv[n, :, :head_cols] = projected[1]
        kv[n, :, head_cols:] = projected[2]
        sums = [(jnp.zeros((rows, HEAD_DIM), F32), jnp.zeros((rows, 1), F32))] * local_heads

        def attend_group(base):
            for h in range(local_heads):
                vcols = slice(head_cols + h * HEAD_DIM, head_cols + (h + 1) * HEAD_DIM)
                keys = kv[pl.ds(base, plane), :, head_at[h]].reshape(group, HEAD_DIM)
                values = kv[pl.ds(base, plane), :, vcols].reshape(group, HEAD_DIM)
                sums[h] = attend(projected[0][:, head_at[h]], keys, values, sums[h])

        gather(kv, kv_sems, attend_group)
        heads = [(a / b).astype(BF) for a, b in sums]
    heads_out = heads[0] if len(heads) == 1 else jnp.concatenate(heads, -1)
    half = width // 2
    mixed_state = stream + sum_over_t(
        1,
        [
            lambda: dot(heads_out, out_v[:, :half]),
            lambda: dot(heads_out, out_v[:, half:]),
        ],
    )

    mlp_in = normed(mixed_state, mg_ref[...]).astype(BF)
    loads[3].wait()
    tile = min(512, up_v.shape[1])
    for i in range(up_v.shape[1] // tile):
        cols = slice(i * tile, (i + 1) * tile)
        hid[:, cols] = jax.nn.gelu(dot(mlp_in, up_v[:, cols])).astype(BF)
    loads[4].wait()
    final_state = mixed_state + sum_over_t(
        2,
        [
            lambda: dot(hid[...], down_v[:, :half]),
            lambda: dot(hid[...], down_v[:, half:]),
        ],
    )
    latents = normed(final_state, fg_ref[...]).astype(BF)
    lat_out[...] = latents
    lat[n] = latents
    loads[5].wait()
    sums = [jnp.zeros((1, neurons), F32)] * 2

    def read_out(base):
        piece = lat[pl.ds(base, plane)].reshape(group, width)
        at = pl.multiple_of(base * rows, group)
        log_rate = dot_nt(piece, readout_v[...]) + bias_ref[...]
        observed = spikes_v[pl.ds(at, group), :].astype(F32)
        sums[0] = sums[0] + jnp.sum(observed * log_rate - jnp.exp(log_rate), 0, keepdims=True)
        sums[1] = sums[1] + jnp.sum(observed, 0, keepdims=True)

    gather(lat, lat_sems, read_out)
    model_ll, counts = sums
    held = held_ref[...]
    heldout = (1 - held).astype(F32)
    null_ll = counts * jnp.log((counts + 1.0) / frames) - (counts + 1.0)
    gained = heldout * (model_ll - null_ll)
    bits_out[...] = gained / (math.log(2.0) * (counts + 1.0))
    score = jnp.sum(gained, -1, keepdims=True)
    spike_sum = jnp.sum(heldout * counts, -1, keepdims=True)
    lane = lax.broadcasted_iota(jnp.int32, (8, 128), 1)
    total = jnp.where(lane == 0, score, jnp.where(lane == 1, spike_sum, 0.0))

    base = 0
    for size, here, peer_of in (
        (plane, m * 2 + c, plane_peer),
        (line, o * t_size + t, line_peer),
    ):
        fin[base + here] = total
        cps = [
            send(fin.at[base + here], fin.at[base + here], fin_sems, (base + d,), peer_of(d))
            for d in range(1, size)
        ]
        if base:
            for cp in sent:
                cp.wait_send()
        for cp in cps:
            cp.wait_recv()
        total = fin[base]
        for i in range(1, size):
            total = total + fin[base + i]
        base += size
    score = jnp.sum(jnp.where(lane == 0, total, 0.0), -1, keepdims=True)
    spike_sum = jnp.sum(jnp.where(lane == 1, total, 0.0), -1, keepdims=True)
    tot_out[...] = jnp.broadcast_to(score / (math.log(2.0) * (1.0 + spike_sum)), (8, 128))


def hand_over(lat_ref, bits_ref, tot_ref, lat_out, bits_out, tot_out):
    lat_out[...] = lat_ref[...]
    bits_out[...] = bits_ref[...]
    tot_out[...] = tot_ref[0:1, 0:1]


def on_device(
    n_size,
    t_size,
    spikes,
    held_in,
    readin_weight,
    qkv_weight,
    out_weight,
    up_weight,
    down_weight,
    norm_gain,
    mlp_gain,
    final_gain,
    readout_weight,
    readout_bias,
):
    frames, neurons = spikes.shape
    width = readin_weight.shape[1]
    rows = frames // n_size
    mid = n_size // (2 * OUTER)
    head_cols = qkv_weight.shape[2]
    qkv = qkv_weight.transpose(1, 0, 2)
    row = lambda v: v.reshape(1, -1)
    vmem = pl.BlockSpec(memory_space=pltpu.VMEM)
    hbm = pl.BlockSpec(memory_space=pltpu.HBM)
    dma = pltpu.SemaphoreType.DMA
    by_head = head_cols == OUTER * HEAD_DIM
    kv_shape = (
        (2 * mid, OUTER, rows, 3 * HEAD_DIM) if by_head else (n_size, rows, 2 * head_cols)
    )
    n_kv = 2 * OUTER + 2 * mid if by_head else n_size
    n_fin = 2 * mid + t_size * OUTER
    latents, bits, total = pl.pallas_call(
        functools.partial(kernel, n_size, t_size),
        out_shape=(
            jax.ShapeDtypeStruct((rows, width), BF),
            jax.ShapeDtypeStruct((1, neurons), F32),
            jax.ShapeDtypeStruct((8, 128), F32),
        ),
        in_specs=[hbm] * 12,
        out_specs=(vmem, vmem, vmem),
        scratch_shapes=[
            pltpu.VMEM(spikes.shape, jnp.int32),
            pltpu.VMEM(readin_weight.shape, BF),
            pltpu.VMEM(qkv.shape, BF),
            pltpu.VMEM(out_weight.shape, BF),
            pltpu.VMEM(up_weight.shape, BF),
            pltpu.VMEM(down_weight.shape, BF),
            pltpu.VMEM(readout_weight.shape, BF),
            pltpu.VMEM((1, neurons), jnp.int32),
            pltpu.VMEM((1, width), F32),
            pltpu.VMEM((1, width), F32),
            pltpu.VMEM((1, width), F32),
            pltpu.VMEM((1, neurons), F32),
            dma((10,)),
            dma((OUTER + 4,)),
            pltpu.VMEM((OUTER, mid, 2, rows, width), F32),
            pltpu.VMEM((OUTER, mid, rows, width), BF),
            pltpu.VMEM((OUTER, mid, rows, width), BF),
            pltpu.VMEM((OUTER, rows, width), F32),
            pltpu.VMEM((OUTER, mid, rows, width), BF),
            pltpu.VMEM((OUTER, mid, rows, width), BF),
            pltpu.VMEM((OUTER, rows, width), BF),
            pltpu.VMEM((OUTER, rows, width), BF),
            pltpu.VMEM((3, t_size, rows, width), BF),
            pltpu.VMEM(kv_shape, BF),
            pltpu.VMEM((OUTER, rows, 3 * HEAD_DIM), BF),
            pltpu.VMEM((OUTER, rows, HEAD_DIM), BF),
            pltpu.VMEM((OUTER, rows, HEAD_DIM), BF),
            pltpu.VMEM((n_size, rows, width), BF),
            pltpu.VMEM((rows, up_weight.shape[1]), BF),
            pltpu.VMEM((n_fin, 8, 128), F32),
            dma((2, OUTER)),
            dma((2, OUTER * mid)),
            dma((2, OUTER)),
            dma((2, 3, 2, t_size)),
            dma((2, n_kv)),
            dma((2, n_size)),
            dma((2, n_fin)),
        ],
        compiler_params=pltpu.CompilerParams(
            collective_id=0, has_side_effects=True, vmem_limit_bytes=60 * 1024 * 1024
        ),
        cost_estimate=pl.CostEstimate(
            flops=4 * frames * neurons * width,
            bytes_accessed=20 * 1024 * 1024,
            transcendentals=frames * neurons,
        ),
    )(
        spikes,
        row(held_in),
        readin_weight,
        qkv,
        out_weight,
        up_weight,
        down_weight,
        row(norm_gain),
        row(mlp_gain),
        row(final_gain),
        readout_weight,
        row(readout_bias),
    )
    latents, bits, total = pl.pallas_call(
        hand_over,
        out_shape=(
            jax.ShapeDtypeStruct((rows, width), BF),
            jax.ShapeDtypeStruct((1, neurons), F32),
            jax.ShapeDtypeStruct((1, 1), F32),
        ),
        in_specs=[vmem] * 3,
        out_specs=(vmem, vmem, vmem),
        compiler_params=pltpu.CompilerParams(vmem_limit_bytes=60 * 1024 * 1024),
    )(latents, bits, total)
    return latents, bits.reshape(neurons), total.reshape(())


def solution(mesh):
    in_specs = (
        P(None, ("neur", "tm")),
        P(("neur", "tm")),
        P(("neur", "tm"), None),
        P(None, None, "tm"),
        P("tm", None),
        P(None, "tm"),
        P("tm", None),
        P(),
        P(),
        P(),
        P(("neur", "tm"), None),
        P(("neur", "tm")),
    )
    out_specs = (P("neur", None), P(("neur", "tm")), P())
    return jax.shard_map(
        functools.partial(on_device, mesh.shape["neur"], mesh.shape["tm"]),
        mesh=mesh,
        in_specs=in_specs,
        out_specs=out_specs,
        check_vma=False,
    )
```

```python
import functools
import math

import jax
import jax.numpy as jnp
from jax import lax
from jax.experimental import pallas as pl
from jax.experimental.pallas import tpu as pltpu
from jax.sharding import PartitionSpec as P

HEAD_DIM = 128
OUTER = 4
MESH = pl.DeviceIdType.MESH
BF = jnp.bfloat16
F32 = jnp.float32


def normed(values, gain_vec):
    return values * lax.rsqrt(jnp.mean(values * values, -1, keepdims=True) + 1e-05) * gain_vec


def dot(a, b):
    return jnp.dot(a, b, preferred_element_type=F32)


def dot_nt(a, b):
    return lax.dot_general(a, b, (((1,), (1,)), ((), ())), preferred_element_type=F32)


def kernel(
    n_size,
    t_size,
    spikes_h,
    held_h,
    readin_h,
    qkv_h,
    out_h,
    up_h,
    down_h,
    ng_h,
    mg_h,
    fg_h,
    readout_h,
    bias_h,
    lat_out,
    bits_out,
    tot_out,
    spikes_v,
    readin_v,
    qkv_v,
    out_v,
    up_v,
    down_v,
    readout_v,
    held_ref,
    ng_ref,
    mg_ref,
    fg_ref,
    bias_ref,
    load_sems,
    spike_sems,
    pp,
    core_s,
    core_r,
    s1,
    mid_s,
    mid_r,
    out_s,
    out_r,
    tsum,
    kv,
    pieces,
    done_s,
    done_r,
    lat,
    hid,
    fin,
    core_sems,
    mid_sems,
    outer_sems,
    t_sems,
    kv_sems,
    lat_sems,
    fin_sems,
):
    mid_size = n_size // (2 * OUTER)
    frames, neurons = spikes_v.shape
    rows = frames // n_size
    width = readin_v.shape[1]
    head_cols = out_v.shape[0]
    group = 2 * mid_size * rows
    n = lax.axis_index("neur")
    t = lax.axis_index("tm")
    c = lax.rem(n, 2)
    m = lax.rem(lax.div(n, 2), mid_size)
    o = lax.div(n, 2 * mid_size)

    def nid(oo, mm, cc):
        return (oo * mid_size + mm) * 2 + cc

    def rot(v, d, size):
        return lax.rem(v + d, size)

    def core_peer():
        return (nid(o, m, 1 - c), t)

    def mid_peer(d):
        return (nid(o, rot(m, d, mid_size), c), t)

    def outer_peer(d):
        return (nid(rot(o, d, OUTER), m, c), t)

    def t_peer(d):
        return (n, rot(t, d, t_size))

    loads = []
    for i, (src, dst) in enumerate(
        (
            (held_h, held_ref),
            (qkv_h, qkv_v),
            (out_h, out_v),
            (up_h, up_v),
            (down_h, down_v),
            (readout_h, readout_v),
            (ng_h, ng_ref),
            (mg_h, mg_ref),
            (fg_h, fg_ref),
            (bias_h, bias_ref),
        )
    ):
        loads.append(pltpu.make_async_copy(src, dst, load_sems.at[i]))
    order = [2, 1, 3, 0]
    starts = {d: pl.multiple_of(rot(o, d, OUTER) * group, group) for d in order}
    spike_loads = {}
    for d in order:
        at = pl.ds(starts[d], group)
        spike_loads[d] = pltpu.make_async_copy(
            spikes_h.at[at, :], spikes_v.at[at, :], spike_sems.at[d]
        )
    quarter = readin_v.shape[0] // 4
    readin_loads = []
    for i in range(4):
        at = pl.ds(i * quarter, quarter)
        readin_loads.append(
            pltpu.make_async_copy(readin_h.at[at, :], readin_v.at[at, :], spike_sems.at[OUTER + i])
        )
    loads[0].start()
    spike_loads[order[0]].start()
    for cp in readin_loads:
        cp.start()
    for d in order[1:]:
        spike_loads[d].start()

    plane = 2 * mid_size
    line = OUTER * t_size

    def plane_peer(d):
        at = rot(m * 2 + c, d, plane)
        return (o * plane + at, t)

    def line_peer(d):
        at = rot(o * t_size + t, d, line)
        return (nid(lax.div(at, t_size), m, c), lax.rem(at, t_size))

    peers = [plane_peer(d) for d in range(1, plane)]
    peers += [line_peer(d) for d in range(1, line)]
    barrier = pltpu.get_barrier_semaphore()
    for peer in peers:
        pl.semaphore_signal(barrier, inc=1, device_id=peer, device_id_type=MESH)

    sent = []

    def send(src, dst, sems, index, peer):
        cp = pltpu.make_async_remote_copy(
            src_ref=src,
            dst_ref=dst,
            send_sem=sems.at[(0,) + index],
            recv_sem=sems.at[(1,) + index],
            device_id=peer,
            device_id_type=MESH,
        )
        cp.start()
        sent.append(cp)
        return cp

    def sum_over_t(which, pieces):
        wide = width // len(pieces)
        cps = []
        for k, piece in enumerate(pieces):
            cols = slice(k * wide, (k + 1) * wide)
            tsum[which, t, :, cols] = piece().astype(BF)
            for d in range(1, t_size):
                part = tsum.at[which, t, :, cols]
                cps.append(send(part, part, t_sems, (which, k, d), t_peer(d)))
        for cp in cps:
            cp.wait_recv()
        total = tsum[which, 0].astype(F32)
        for i in range(1, t_size):
            total = total + tsum[which, i].astype(F32)
        return total

    def gather(buf, sems, use):
        cps = {}

        def push(do, dm, dc):
            if dc:
                own_m = rot(m, mid_size - dm, mid_size)
                own_o = rot(o, OUTER - do, OUTER)
                peer = core_peer()
            elif dm:
                own_m, own_o = m, rot(o, OUTER - do, OUTER)
                peer = mid_peer(dm)
            else:
                own_m, own_o = m, o
                peer = outer_peer(do)
            block = nid(own_o, own_m, c)
            cps[do, dm, dc] = send(
                buf.at[block], buf.at[block], sems, ((do * mid_size + dm) * 2 + dc,), peer
            )

        def to_mid(do):
            if do:
                cps[do, 0, 0].wait_recv()
            for d in range(1, mid_size):
                push(do, d, 0)
            push(do, 0, 1)

        def to_core(do):
            for d in range(1, mid_size):
                cps[do, d, 0].wait_recv()
                push(do, d, 1)

        def finish(do):
            for d in range(mid_size):
                cps[do, d, 1].wait_recv()
            use(rot(o, OUTER - do, OUTER) * plane)

        push(1, 0, 0)
        push(3, 0, 0)
        to_mid(0)
        to_core(0)
        for d in (1, 3):
            cps[d, 0, 0].wait_send()
            sent[:] = [cp for cp in sent if cp is not cps[d, 0, 0]]
        push(2, 0, 0)
        to_mid(1)
        to_mid(3)
        finish(0)
        to_core(1)
        to_core(3)
        to_mid(2)
        finish(1)
        to_core(2)
        finish(3)
        finish(2)

    core_cps, mid_cps, outer_cps = {}, {}, {}

    def read_in(d):
        spike_loads[d].wait()
        masked = (spikes_v[pl.ds(starts[d], group), :] * held_ref[...]).astype(F32).astype(BF)
        pp[d] = dot(masked, readin_v[...]).reshape(mid_size, 2, rows, width)
        for i in range(mid_size):
            core_s[d, i] = pp[d, i, 1 - c].astype(BF)
        if d == order[0]:
            pl.semaphore_wait(barrier, len(peers))
        core_cps[d] = send(core_s.at[d], core_r.at[d], core_sems, (d,), core_peer())

    def over_mid(d):
        core_cps[d].wait_recv()
        for dm in list(range(1, mid_size)) + [0]:
            mm = rot(m, dm, mid_size)
            value = pp[d, mm, c] + core_r[d, mm].astype(F32)
            if dm:
                mid_s[d, dm] = value.astype(BF)
                mid_cps[d, dm] = send(
                    mid_s.at[d, dm], mid_r.at[d, dm], mid_sems, (d * mid_size + dm,), mid_peer(dm)
                )
            else:
                s1[d] = value

    def over_outer(d):
        value = s1[d]
        for dm in range(1, mid_size):
            mid_cps[d, dm].wait_recv()
            value = value + mid_r[d, dm].astype(F32)
        if d:
            out_s[d] = value.astype(BF)
            outer_cps[d] = send(out_s.at[d], out_r.at[d], outer_sems, (d,), outer_peer(d))
        return value

    loads[0].wait()
    for cp in readin_loads:
        cp.wait()
    read_in(2)
    for cp in loads[1:]:
        cp.start()
    read_in(1)
    over_mid(2)
    read_in(3)
    over_mid(1)
    read_in(0)
    over_mid(3)
    over_outer(2)
    over_mid(0)
    over_outer(1)
    over_outer(3)
    value = over_outer(0)
    for d in (2, 1, 3):
        outer_cps[d].wait_recv()
        value = value + out_r[d].astype(F32)
    stream = sum_over_t(0, [lambda: value])

    for cp in loads[6:]:
        cp.wait()
    attn_in = normed(stream, ng_ref[...]).astype(BF)
    loads[1].wait()

    def project(i):
        return dot(attn_in, qkv_v[i]).astype(BF)

    scaling = 1.0 / math.sqrt(HEAD_DIM)
    local_heads = head_cols // HEAD_DIM
    head_at = [slice(h * HEAD_DIM, (h + 1) * HEAD_DIM) for h in range(local_heads)]

    def attend(query, keys, values, sums):
        weights = jnp.exp(dot_nt(query, keys) * scaling)
        return (
            sums[0] + dot(weights.astype(BF), values),
            sums[1] + jnp.sum(weights, -1, keepdims=True),
        )

    if local_heads == OUTER:
        spot = m * 2 + c
        key_value = slice(HEAD_DIM, 3 * HEAD_DIM)

        def turn(cols, base):
            return {
                d: send(
                    pieces.at[rot(o, d, OUTER), :, cols],
                    kv.at[spot, o, :, cols],
                    kv_sems,
                    (base + d,),
                    outer_peer(d),
                )
                for d in (2, 1, 3)
            }

        spread = {}

        def into_plane(do):
            there = rot(o, OUTER - do, OUTER)
            for d in range(1, plane):
                part = kv.at[spot, there, :, key_value]
                spread[do, d] = send(
                    part, part, kv_sems, (2 * OUTER + do * plane + d,), plane_peer(d)
                )

        for i in (1, 2):
            piece = project(i)
            for h in range(OUTER):
                pieces[h, :, head_at[i]] = piece[:, head_at[h]]
        turned = turn(key_value, 0)
        kv[spot, o, :, key_value] = pieces[o, :, key_value]
        into_plane(0)
        piece = project(0)
        for h in range(OUTER):
            pieces[h, :, head_at[0]] = piece[:, head_at[h]]
        turned_query = turn(head_at[0], OUTER)
        kv[spot, o, :, head_at[0]] = pieces[o, :, head_at[0]]
        for d in (1, 3, 2):
            turned[d].wait_recv()
            into_plane(d)
        for d in (1, 3, 2):
            turned_query[d].wait_recv()
        query = kv[spot, :, :, head_at[0]].reshape(OUTER * rows, HEAD_DIM)
        sums = (jnp.zeros(query.shape, F32), jnp.zeros((OUTER * rows, 1), F32))
        for d in range(plane):
            if d:
                for do in range(OUTER):
                    spread[do, d].wait_recv()
            there = rot(spot, plane - d, plane)
            keys = kv[there, :, :, head_at[1]].reshape(OUTER * rows, HEAD_DIM)
            values = kv[there, :, :, head_at[2]].reshape(OUTER * rows, HEAD_DIM)
            sums = attend(query, keys, values, sums)
        done_s[...] = (sums[0] / sums[1]).astype(BF).reshape(OUTER, rows, HEAD_DIM)
        back = [
            send(
                done_s.at[rot(o, d, OUTER)],
                done_r.at[o],
                kv_sems,
                ((2 + plane) * OUTER + d,),
                outer_peer(d),
            )
            for d in (2, 1, 3)
        ]
        done_r[o] = done_s[o]
        for cp in back:
            cp.wait_recv()
        heads = [done_r[h] for h in range(OUTER)]
    else:
        projected = [project(i) for i in range(3)]
        kv[n, :, :head_cols] = projected[1]
        kv[n, :, head_cols:] = projected[2]
        sums = [(jnp.zeros((rows, HEAD_DIM), F32), jnp.zeros((rows, 1), F32))] * local_heads

        def attend_group(base):
            for h in range(local_heads):
                vcols = slice(head_cols + h * HEAD_DIM, head_cols + (h + 1) * HEAD_DIM)
                keys = kv[pl.ds(base, plane), :, head_at[h]].reshape(group, HEAD_DIM)
                values = kv[pl.ds(base, plane), :, vcols].reshape(group, HEAD_DIM)
                sums[h] = attend(projected[0][:, head_at[h]], keys, values, sums[h])

        gather(kv, kv_sems, attend_group)
        heads = [(a / b).astype(BF) for a, b in sums]
    loads[2].wait()
    heads_out = heads[0] if len(heads) == 1 else jnp.concatenate(heads, -1)
    half = width // 2
    mixed_state = stream + sum_over_t(
        1,
        [
            lambda: dot(heads_out, out_v[:, :half]),
            lambda: dot(heads_out, out_v[:, half:]),
        ],
    )

    mlp_in = normed(mixed_state, mg_ref[...]).astype(BF)
    loads[3].wait()
    tile = min(512, up_v.shape[1])
    for i in range(up_v.shape[1] // tile):
        cols = slice(i * tile, (i + 1) * tile)
        hid[:, cols] = jax.nn.gelu(dot(mlp_in, up_v[:, cols])).astype(BF)
    loads[4].wait()
    final_state = mixed_state + sum_over_t(
        2,
        [
            lambda: dot(hid[...], down_v[:, :half]),
            lambda: dot(hid[...], down_v[:, half:]),
        ],
    )
    latents = normed(final_state, fg_ref[...]).astype(BF)
    lat_out[...] = latents
    lat[n] = latents
    loads[5].wait()
    sums = [jnp.zeros((1, neurons), F32)] * 2

    def read_out(base):
        piece = lat[pl.ds(base, plane)].reshape(group, width)
        at = pl.multiple_of(base * rows, group)
        log_rate = dot_nt(piece, readout_v[...]) + bias_ref[...]
        observed = spikes_v[pl.ds(at, group), :].astype(F32)
        sums[0] = sums[0] + jnp.sum(observed * log_rate - jnp.exp(log_rate), 0, keepdims=True)
        sums[1] = sums[1] + jnp.sum(observed, 0, keepdims=True)

    gather(lat, lat_sems, read_out)
    model_ll, counts = sums
    held = held_ref[...]
    heldout = (1 - held).astype(F32)
    null_ll = counts * jnp.log((counts + 1.0) / frames) - (counts + 1.0)
    gained = heldout * (model_ll - null_ll)
    bits_out[...] = gained / (math.log(2.0) * (counts + 1.0))
    score = jnp.sum(gained, -1, keepdims=True)
    spike_sum = jnp.sum(heldout * counts, -1, keepdims=True)
    lane = lax.broadcasted_iota(jnp.int32, (8, 128), 1)
    total = jnp.where(lane == 0, score, jnp.where(lane == 1, spike_sum, 0.0))

    base = 0
    for size, here, peer_of in (
        (plane, m * 2 + c, plane_peer),
        (line, o * t_size + t, line_peer),
    ):
        fin[base + here] = total
        cps = [
            send(fin.at[base + here], fin.at[base + here], fin_sems, (base + d,), peer_of(d))
            for d in range(1, size)
        ]
        if base:
            for cp in sent:
                cp.wait_send()
        for cp in cps:
            cp.wait_recv()
        total = fin[base]
        for i in range(1, size):
            total = total + fin[base + i]
        base += size
    score = jnp.sum(jnp.where(lane == 0, total, 0.0), -1, keepdims=True)
    spike_sum = jnp.sum(jnp.where(lane == 1, total, 0.0), -1, keepdims=True)
    tot_out[...] = jnp.broadcast_to(score / (math.log(2.0) * (1.0 + spike_sum)), (8, 128))


def hand_over(lat_ref, bits_ref, tot_ref, lat_out, bits_out, tot_out):
    lat_out[...] = lat_ref[...]
    bits_out[...] = bits_ref[...]
    tot_out[...] = tot_ref[0:1, 0:1]


def on_device(
    n_size,
    t_size,
    spikes,
    held_in,
    readin_weight,
    qkv_weight,
    out_weight,
    up_weight,
    down_weight,
    norm_gain,
    mlp_gain,
    final_gain,
    readout_weight,
    readout_bias,
):
    frames, neurons = spikes.shape
    width = readin_weight.shape[1]
    rows = frames // n_size
    mid = n_size // (2 * OUTER)
    head_cols = qkv_weight.shape[2]
    qkv = qkv_weight.transpose(1, 0, 2)
    row = lambda v: v.reshape(1, -1)
    vmem = pl.BlockSpec(memory_space=pltpu.VMEM)
    hbm = pl.BlockSpec(memory_space=pltpu.HBM)
    dma = pltpu.SemaphoreType.DMA
    by_head = head_cols == OUTER * HEAD_DIM
    kv_shape = (
        (2 * mid, OUTER, rows, 3 * HEAD_DIM) if by_head else (n_size, rows, 2 * head_cols)
    )
    n_kv = (3 + 2 * mid) * OUTER if by_head else n_size
    n_fin = 2 * mid + t_size * OUTER
    latents, bits, total = pl.pallas_call(
        functools.partial(kernel, n_size, t_size),
        out_shape=(
            jax.ShapeDtypeStruct((rows, width), BF),
            jax.ShapeDtypeStruct((1, neurons), F32),
            jax.ShapeDtypeStruct((8, 128), F32),
        ),
        in_specs=[hbm] * 12,
        out_specs=(vmem, vmem, vmem),
        scratch_shapes=[
            pltpu.VMEM(spikes.shape, jnp.int32),
            pltpu.VMEM(readin_weight.shape, BF),
            pltpu.VMEM(qkv.shape, BF),
            pltpu.VMEM(out_weight.shape, BF),
            pltpu.VMEM(up_weight.shape, BF),
            pltpu.VMEM(down_weight.shape, BF),
            pltpu.VMEM(readout_weight.shape, BF),
            pltpu.VMEM((1, neurons), jnp.int32),
            pltpu.VMEM((1, width), F32),
            pltpu.VMEM((1, width), F32),
            pltpu.VMEM((1, width), F32),
            pltpu.VMEM((1, neurons), F32),
            dma((10,)),
            dma((OUTER + 4,)),
            pltpu.VMEM((OUTER, mid, 2, rows, width), F32),
            pltpu.VMEM((OUTER, mid, rows, width), BF),
            pltpu.VMEM((OUTER, mid, rows, width), BF),
            pltpu.VMEM((OUTER, rows, width), F32),
            pltpu.VMEM((OUTER, mid, rows, width), BF),
            pltpu.VMEM((OUTER, mid, rows, width), BF),
            pltpu.VMEM((OUTER, rows, width), BF),
            pltpu.VMEM((OUTER, rows, width), BF),
            pltpu.VMEM((3, t_size, rows, width), BF),
            pltpu.VMEM(kv_shape, BF),
            pltpu.VMEM((OUTER, rows, 3 * HEAD_DIM), BF),
            pltpu.VMEM((OUTER, rows, HEAD_DIM), BF),
            pltpu.VMEM((OUTER, rows, HEAD_DIM), BF),
            pltpu.VMEM((n_size, rows, width), BF),
            pltpu.VMEM((rows, up_weight.shape[1]), BF),
            pltpu.VMEM((n_fin, 8, 128), F32),
            dma((2, OUTER)),
            dma((2, OUTER * mid)),
            dma((2, OUTER)),
            dma((2, 3, 2, t_size)),
            dma((2, n_kv)),
            dma((2, n_size)),
            dma((2, n_fin)),
        ],
        compiler_params=pltpu.CompilerParams(
            collective_id=0, has_side_effects=True, vmem_limit_bytes=60 * 1024 * 1024
        ),
        cost_estimate=pl.CostEstimate(
            flops=4 * frames * neurons * width,
            bytes_accessed=20 * 1024 * 1024,
            transcendentals=frames * neurons,
        ),
    )(
        spikes,
        row(held_in),
        readin_weight,
        qkv,
        out_weight,
        up_weight,
        down_weight,
        row(norm_gain),
        row(mlp_gain),
        row(final_gain),
        readout_weight,
        row(readout_bias),
    )
    latents, bits, total = pl.pallas_call(
        hand_over,
        out_shape=(
            jax.ShapeDtypeStruct((rows, width), BF),
            jax.ShapeDtypeStruct((1, neurons), F32),
            jax.ShapeDtypeStruct((1, 1), F32),
        ),
        in_specs=[vmem] * 3,
        out_specs=(vmem, vmem, vmem),
        compiler_params=pltpu.CompilerParams(vmem_limit_bytes=60 * 1024 * 1024),
    )(latents, bits, total)
    return latents, bits.reshape(neurons), total.reshape(())


def solution(mesh):
    in_specs = (
        P(None, ("neur", "tm")),
        P(("neur", "tm")),
        P(("neur", "tm"), None),
        P(None, None, "tm"),
        P("tm", None),
        P(None, "tm"),
        P("tm", None),
        P(),
        P(),
        P(),
        P(("neur", "tm"), None),
        P(("neur", "tm")),
    )
    out_specs = (P("neur", None), P(("neur", "tm")), P())
    return jax.shard_map(
        functools.partial(on_device, mesh.shape["neur"], mesh.shape["tm"]),
        mesh=mesh,
        in_specs=in_specs,
        out_specs=out_specs,
        check_vma=False,
    )
```

```python
import functools
import math

import jax
import jax.numpy as jnp
from jax import lax
from jax.experimental import pallas as pl
from jax.experimental.pallas import tpu as pltpu
from jax.sharding import PartitionSpec as P

HEAD_DIM = 128
OUTER = 4
TILE = 256
MESH = pl.DeviceIdType.MESH
BF = jnp.bfloat16
F32 = jnp.float32


def normed(values, gain_vec):
    return values * lax.rsqrt(jnp.mean(values * values, -1, keepdims=True) + 1e-05) * gain_vec


def dot(a, b):
    return jnp.dot(a, b, preferred_element_type=F32)


def dot_nt(a, b):
    return lax.dot_general(a, b, (((1,), (1,)), ((), ())), preferred_element_type=F32)


def kernel(
    n_size,
    t_size,
    spikes_h,
    held_h,
    readin_h,
    qkv_h,
    out_h,
    up_h,
    down_h,
    ng_h,
    mg_h,
    fg_h,
    readout_h,
    bias_h,
    lat_out,
    bits_out,
    tot_out,
    spikes_v,
    readin_v,
    qkv_v,
    out_v,
    up_v,
    down_v,
    readout_v,
    held_ref,
    ng_ref,
    mg_ref,
    fg_ref,
    bias_ref,
    load_sems,
    spike_sems,
    pp,
    core_s,
    core_r,
    s1,
    mid_s,
    mid_r,
    out_s,
    out_r,
    tsum,
    kv,
    pieces,
    done_s,
    done_r,
    lat,
    hid,
    fin,
    mask_v,
    acc,
    core_sems,
    mid_sems,
    outer_sems,
    t_sems,
    kv_sems,
    lat_sems,
    fin_sems,
):
    mid_size = n_size // (2 * OUTER)
    frames, neurons = spikes_v.shape
    rows = frames // n_size
    width = readin_v.shape[1]
    head_cols = out_v.shape[0]
    group = 2 * mid_size * rows
    n = lax.axis_index("neur")
    t = lax.axis_index("tm")
    c = lax.rem(n, 2)
    m = lax.rem(lax.div(n, 2), mid_size)
    o = lax.div(n, 2 * mid_size)

    def nid(oo, mm, cc):
        return (oo * mid_size + mm) * 2 + cc

    def rot(v, d, size):
        return lax.rem(v + d, size)

    def core_peer():
        return (nid(o, m, 1 - c), t)

    def mid_peer(d):
        return (nid(o, rot(m, d, mid_size), c), t)

    def outer_peer(d):
        return (nid(rot(o, d, OUTER), m, c), t)

    def t_peer(d):
        return (n, rot(t, d, t_size))

    loads = []
    for i, (src, dst) in enumerate(
        (
            (held_h, held_ref),
            (qkv_h, qkv_v),
            (out_h, out_v),
            (up_h, up_v),
            (down_h, down_v),
            (readout_h, readout_v),
            (ng_h, ng_ref),
            (mg_h, mg_ref),
            (fg_h, fg_ref),
            (bias_h, bias_ref),
        )
    ):
        loads.append(pltpu.make_async_copy(src, dst, load_sems.at[i]))
    order = [2, 1, 3, 0]
    starts = {d: pl.multiple_of(rot(o, d, OUTER) * group, group) for d in order}
    spike_loads = {}
    for d in order:
        at = pl.ds(starts[d], group)
        spike_loads[d] = pltpu.make_async_copy(
            spikes_h.at[at, :], spikes_v.at[at, :], spike_sems.at[d]
        )
    quarter = readin_v.shape[0] // 4
    readin_loads = []
    for i in range(4):
        at = pl.ds(i * quarter, quarter)
        readin_loads.append(
            pltpu.make_async_copy(readin_h.at[at, :], readin_v.at[at, :], spike_sems.at[OUTER + i])
        )
    loads[0].start()
    spike_loads[order[0]].start()
    for cp in readin_loads:
        cp.start()
    for d in order[1:]:
        spike_loads[d].start()

    plane = 2 * mid_size
    line = OUTER * t_size

    def plane_peer(d):
        at = rot(m * 2 + c, d, plane)
        return (o * plane + at, t)

    def line_peer(d):
        at = rot(o * t_size + t, d, line)
        return (nid(lax.div(at, t_size), m, c), lax.rem(at, t_size))

    peers = [plane_peer(d) for d in range(1, plane)]
    peers += [line_peer(d) for d in range(1, line)]
    barrier = pltpu.get_barrier_semaphore()
    for peer in peers:
        pl.semaphore_signal(barrier, inc=1, device_id=peer, device_id_type=MESH)

    sent = []

    def send(src, dst, sems, index, peer):
        cp = pltpu.make_async_remote_copy(
            src_ref=src,
            dst_ref=dst,
            send_sem=sems.at[(0,) + index],
            recv_sem=sems.at[(1,) + index],
            device_id=peer,
            device_id_type=MESH,
        )
        cp.start()
        sent.append(cp)
        return cp

    def sum_over_t(which, pieces):
        wide = width // len(pieces)
        cps = []
        for k, piece in enumerate(pieces):
            cols = slice(k * wide, (k + 1) * wide)
            tsum[which, t, :, cols] = piece().astype(BF)
            for d in range(1, t_size):
                part = tsum.at[which, t, :, cols]
                cps.append(send(part, part, t_sems, (which, k, d), t_peer(d)))
        for cp in cps:
            cp.wait_recv()
        total = tsum[which, 0].astype(F32)
        for i in range(1, t_size):
            total = total + tsum[which, i].astype(F32)
        return total

    def gather(buf, sems, use):
        cps = {}

        def push(do, dm, dc):
            if dc:
                own_m = rot(m, mid_size - dm, mid_size)
                own_o = rot(o, OUTER - do, OUTER)
                peer = core_peer()
            elif dm:
                own_m, own_o = m, rot(o, OUTER - do, OUTER)
                peer = mid_peer(dm)
            else:
                own_m, own_o = m, o
                peer = outer_peer(do)
            block = nid(own_o, own_m, c)
            cps[do, dm, dc] = send(
                buf.at[block], buf.at[block], sems, ((do * mid_size + dm) * 2 + dc,), peer
            )

        def to_mid(do):
            if do:
                cps[do, 0, 0].wait_recv()
            for d in range(1, mid_size):
                push(do, d, 0)
            push(do, 0, 1)

        def to_core(do):
            for d in range(1, mid_size):
                cps[do, d, 0].wait_recv()
                push(do, d, 1)

        def finish(do):
            for d in range(mid_size):
                cps[do, d, 1].wait_recv()
            use(rot(o, OUTER - do, OUTER) * plane)

        push(1, 0, 0)
        push(3, 0, 0)
        to_mid(0)
        to_core(0)
        for d in (1, 3):
            cps[d, 0, 0].wait_send()
            sent[:] = [cp for cp in sent if cp is not cps[d, 0, 0]]
        push(2, 0, 0)
        to_mid(1)
        to_mid(3)
        finish(0)
        to_core(1)
        to_core(3)
        to_mid(2)
        finish(1)
        to_core(2)
        finish(3)
        finish(2)

    core_cps, mid_cps, outer_cps = {}, {}, {}

    def read_in(d):
        spike_loads[d].wait()
        mask_v[...] = (
            (spikes_v[pl.ds(starts[d], group), :] * held_ref[...]).astype(F32).astype(BF)
        )

        def columns(j, carry):
            cols = pl.ds(pl.multiple_of(j * TILE, TILE), TILE)
            pp[d, :, :, :, cols] = dot(mask_v[...], readin_v[:, cols]).reshape(
                mid_size, 2, rows, TILE
            )
            return carry

        lax.fori_loop(0, width // TILE, columns, 0)
        for i in range(mid_size):
            core_s[d, i] = pp[d, i, 1 - c].astype(BF)
        if d == order[0]:
            pl.semaphore_wait(barrier, len(peers))
        core_cps[d] = send(core_s.at[d], core_r.at[d], core_sems, (d,), core_peer())

    def over_mid(d):
        core_cps[d].wait_recv()
        for dm in list(range(1, mid_size)) + [0]:
            mm = rot(m, dm, mid_size)
            value = pp[d, mm, c] + core_r[d, mm].astype(F32)
            if dm:
                mid_s[d, dm] = value.astype(BF)
                mid_cps[d, dm] = send(
                    mid_s.at[d, dm], mid_r.at[d, dm], mid_sems, (d * mid_size + dm,), mid_peer(dm)
                )
            else:
                s1[d] = value

    def over_outer(d):
        value = s1[d]
        for dm in range(1, mid_size):
            mid_cps[d, dm].wait_recv()
            value = value + mid_r[d, dm].astype(F32)
        if d:
            out_s[d] = value.astype(BF)
            outer_cps[d] = send(out_s.at[d], out_r.at[d], outer_sems, (d,), outer_peer(d))
        return value

    loads[0].wait()
    for cp in readin_loads:
        cp.wait()
    read_in(2)
    for cp in loads[1:]:
        cp.start()
    read_in(1)
    over_mid(2)
    read_in(3)
    over_mid(1)
    read_in(0)
    over_mid(3)
    over_outer(2)
    over_mid(0)
    over_outer(1)
    over_outer(3)
    value = over_outer(0)
    for d in (2, 1, 3):
        outer_cps[d].wait_recv()
        value = value + out_r[d].astype(F32)
    stream = sum_over_t(0, [lambda: value])

    for cp in loads[6:]:
        cp.wait()
    attn_in = normed(stream, ng_ref[...]).astype(BF)
    loads[1].wait()

    def project(i):
        return dot(attn_in, qkv_v[i]).astype(BF)

    scaling = 1.0 / math.sqrt(HEAD_DIM)
    local_heads = head_cols // HEAD_DIM
    head_at = [slice(h * HEAD_DIM, (h + 1) * HEAD_DIM) for h in range(local_heads)]

    def attend(query, keys, values, sums):
        weights = jnp.exp(dot_nt(query, keys) * scaling)
        return (
            sums[0] + dot(weights.astype(BF), values),
            sums[1] + jnp.sum(weights, -1, keepdims=True),
        )

    if local_heads == OUTER:
        spot = m * 2 + c
        key_value = slice(HEAD_DIM, 3 * HEAD_DIM)

        def turn(cols, base):
            return {
                d: send(
                    pieces.at[rot(o, d, OUTER), :, cols],
                    kv.at[spot, o, :, cols],
                    kv_sems,
                    (base + d,),
                    outer_peer(d),
                )
                for d in (2, 1, 3)
            }

        spread = {}

        def into_plane(do):
            there = rot(o, OUTER - do, OUTER)
            for d in range(1, plane):
                part = kv.at[spot, there, :, key_value]
                spread[do, d] = send(
                    part, part, kv_sems, (2 * OUTER + do * plane + d,), plane_peer(d)
                )

        for i in (1, 2):
            piece = project(i)
            for h in range(OUTER):
                pieces[h, :, head_at[i]] = piece[:, head_at[h]]
        turned = turn(key_value, 0)
        kv[spot, o, :, key_value] = pieces[o, :, key_value]
        into_plane(0)
        piece = project(0)
        for h in range(OUTER):
            pieces[h, :, head_at[0]] = piece[:, head_at[h]]
        turned_query = turn(head_at[0], OUTER)
        kv[spot, o, :, head_at[0]] = pieces[o, :, head_at[0]]
        for d in (1, 3, 2):
            turned[d].wait_recv()
            into_plane(d)
        for d in (1, 3, 2):
            turned_query[d].wait_recv()
        query = kv[spot, :, :, head_at[0]].reshape(OUTER * rows, HEAD_DIM)
        sums = (jnp.zeros(query.shape, F32), jnp.zeros((OUTER * rows, 1), F32))
        for d in range(plane):
            if d:
                for do in range(OUTER):
                    spread[do, d].wait_recv()
            there = rot(spot, plane - d, plane)
            keys = kv[there, :, :, head_at[1]].reshape(OUTER * rows, HEAD_DIM)
            values = kv[there, :, :, head_at[2]].reshape(OUTER * rows, HEAD_DIM)
            sums = attend(query, keys, values, sums)
        done_s[...] = (sums[0] / sums[1]).astype(BF).reshape(OUTER, rows, HEAD_DIM)
        back = [
            send(
                done_s.at[rot(o, d, OUTER)],
                done_r.at[o],
                kv_sems,
                ((2 + plane) * OUTER + d,),
                outer_peer(d),
            )
            for d in (2, 1, 3)
        ]
        done_r[o] = done_s[o]
        for cp in back:
            cp.wait_recv()
        heads = [done_r[h] for h in range(OUTER)]
    else:
        projected = [project(i) for i in range(3)]
        kv[n, :, :head_cols] = projected[1]
        kv[n, :, head_cols:] = projected[2]
        sums = [(jnp.zeros((rows, HEAD_DIM), F32), jnp.zeros((rows, 1), F32))] * local_heads

        def attend_group(base):
            for h in range(local_heads):
                vcols = slice(head_cols + h * HEAD_DIM, head_cols + (h + 1) * HEAD_DIM)
                keys = kv[pl.ds(base, plane), :, head_at[h]].reshape(group, HEAD_DIM)
                values = kv[pl.ds(base, plane), :, vcols].reshape(group, HEAD_DIM)
                sums[h] = attend(projected[0][:, head_at[h]], keys, values, sums[h])

        gather(kv, kv_sems, attend_group)
        heads = [(a / b).astype(BF) for a, b in sums]
    loads[2].wait()
    heads_out = heads[0] if len(heads) == 1 else jnp.concatenate(heads, -1)
    half = width // 2
    mixed_state = stream + sum_over_t(
        1,
        [
            lambda: dot(heads_out, out_v[:, :half]),
            lambda: dot(heads_out, out_v[:, half:]),
        ],
    )

    mlp_in = normed(mixed_state, mg_ref[...]).astype(BF)
    loads[3].wait()

    def up_columns(j, carry):
        cols = pl.ds(pl.multiple_of(j * TILE, TILE), TILE)
        hid[:, cols] = jax.nn.gelu(dot(mlp_in, up_v[:, cols])).astype(BF)
        return carry

    lax.fori_loop(0, up_v.shape[1] // TILE, up_columns, 0)
    loads[4].wait()
    final_state = mixed_state + sum_over_t(
        2,
        [
            lambda: dot(hid[...], down_v[:, :half]),
            lambda: dot(hid[...], down_v[:, half:]),
        ],
    )
    latents = normed(final_state, fg_ref[...]).astype(BF)
    lat_out[...] = latents
    lat[n] = latents
    loads[5].wait()
    acc[...] = jnp.zeros(acc.shape, F32)

    def read_out(base):
        at = pl.multiple_of(base * rows, group)

        def columns(j, carry):
            cols = pl.ds(pl.multiple_of(j * TILE, TILE), TILE)
            piece = lat[pl.ds(base, plane)].reshape(group, width)
            log_rate = dot_nt(piece, readout_v[cols, :]) + bias_ref[:, cols]
            observed = spikes_v[pl.ds(at, group), cols].astype(F32)
            acc[0, :, cols] += jnp.sum(observed * log_rate - jnp.exp(log_rate), 0, keepdims=True)
            acc[1, :, cols] += jnp.sum(observed, 0, keepdims=True)
            return carry

        lax.fori_loop(0, neurons // TILE, columns, 0)

    gather(lat, lat_sems, read_out)
    model_ll, counts = acc[0], acc[1]
    held = held_ref[...]
    heldout = (1 - held).astype(F32)
    null_ll = counts * jnp.log((counts + 1.0) / frames) - (counts + 1.0)
    gained = heldout * (model_ll - null_ll)
    bits_out[...] = gained / (math.log(2.0) * (counts + 1.0))
    score = jnp.sum(gained, -1, keepdims=True)
    spike_sum = jnp.sum(heldout * counts, -1, keepdims=True)
    lane = lax.broadcasted_iota(jnp.int32, (8, 128), 1)
    total = jnp.where(lane == 0, score, jnp.where(lane == 1, spike_sum, 0.0))

    base = 0
    for size, here, peer_of in (
        (plane, m * 2 + c, plane_peer),
        (line, o * t_size + t, line_peer),
    ):
        fin[base + here] = total
        cps = [
            send(fin.at[base + here], fin.at[base + here], fin_sems, (base + d,), peer_of(d))
            for d in range(1, size)
        ]
        if base:
            for cp in sent:
                cp.wait_send()
        for cp in cps:
            cp.wait_recv()
        total = fin[base]
        for i in range(1, size):
            total = total + fin[base + i]
        base += size
    score = jnp.sum(jnp.where(lane == 0, total, 0.0), -1, keepdims=True)
    spike_sum = jnp.sum(jnp.where(lane == 1, total, 0.0), -1, keepdims=True)
    tot_out[...] = jnp.broadcast_to(score / (math.log(2.0) * (1.0 + spike_sum)), (8, 128))


def hand_over(lat_ref, bits_ref, tot_ref, lat_out, bits_out, tot_out):
    lat_out[...] = lat_ref[...]
    bits_out[...] = bits_ref[...]
    tot_out[...] = tot_ref[0:1, 0:1]


def on_device(
    n_size,
    t_size,
    spikes,
    held_in,
    readin_weight,
    qkv_weight,
    out_weight,
    up_weight,
    down_weight,
    norm_gain,
    mlp_gain,
    final_gain,
    readout_weight,
    readout_bias,
):
    frames, neurons = spikes.shape
    width = readin_weight.shape[1]
    rows = frames // n_size
    mid = n_size // (2 * OUTER)
    head_cols = qkv_weight.shape[2]
    qkv = qkv_weight.transpose(1, 0, 2)
    row = lambda v: v.reshape(1, -1)
    vmem = pl.BlockSpec(memory_space=pltpu.VMEM)
    hbm = pl.BlockSpec(memory_space=pltpu.HBM)
    dma = pltpu.SemaphoreType.DMA
    by_head = head_cols == OUTER * HEAD_DIM
    kv_shape = (
        (2 * mid, OUTER, rows, 3 * HEAD_DIM) if by_head else (n_size, rows, 2 * head_cols)
    )
    n_kv = (3 + 2 * mid) * OUTER if by_head else n_size
    n_fin = 2 * mid + t_size * OUTER
    latents, bits, total = pl.pallas_call(
        functools.partial(kernel, n_size, t_size),
        out_shape=(
            jax.ShapeDtypeStruct((rows, width), BF),
            jax.ShapeDtypeStruct((1, neurons), F32),
            jax.ShapeDtypeStruct((8, 128), F32),
        ),
        in_specs=[hbm] * 12,
        out_specs=(vmem, vmem, vmem),
        scratch_shapes=[
            pltpu.VMEM(spikes.shape, jnp.int32),
            pltpu.VMEM(readin_weight.shape, BF),
            pltpu.VMEM(qkv.shape, BF),
            pltpu.VMEM(out_weight.shape, BF),
            pltpu.VMEM(up_weight.shape, BF),
            pltpu.VMEM(down_weight.shape, BF),
            pltpu.VMEM(readout_weight.shape, BF),
            pltpu.VMEM((1, neurons), jnp.int32),
            pltpu.VMEM((1, width), F32),
            pltpu.VMEM((1, width), F32),
            pltpu.VMEM((1, width), F32),
            pltpu.VMEM((1, neurons), F32),
            dma((10,)),
            dma((OUTER + 4,)),
            pltpu.VMEM((OUTER, mid, 2, rows, width), F32),
            pltpu.VMEM((OUTER, mid, rows, width), BF),
            pltpu.VMEM((OUTER, mid, rows, width), BF),
            pltpu.VMEM((OUTER, rows, width), F32),
            pltpu.VMEM((OUTER, mid, rows, width), BF),
            pltpu.VMEM((OUTER, mid, rows, width), BF),
            pltpu.VMEM((OUTER, rows, width), BF),
            pltpu.VMEM((OUTER, rows, width), BF),
            pltpu.VMEM((3, t_size, rows, width), BF),
            pltpu.VMEM(kv_shape, BF),
            pltpu.VMEM((OUTER, rows, 3 * HEAD_DIM), BF),
            pltpu.VMEM((OUTER, rows, HEAD_DIM), BF),
            pltpu.VMEM((OUTER, rows, HEAD_DIM), BF),
            pltpu.VMEM((n_size, rows, width), BF),
            pltpu.VMEM((rows, up_weight.shape[1]), BF),
            pltpu.VMEM((n_fin, 8, 128), F32),
            pltpu.VMEM((2 * mid * rows, neurons), BF),
            pltpu.VMEM((2, 1, neurons), F32),
            dma((2, OUTER)),
            dma((2, OUTER * mid)),
            dma((2, OUTER)),
            dma((2, 3, 2, t_size)),
            dma((2, n_kv)),
            dma((2, n_size)),
            dma((2, n_fin)),
        ],
        compiler_params=pltpu.CompilerParams(
            collective_id=0, has_side_effects=True, vmem_limit_bytes=60 * 1024 * 1024
        ),
        cost_estimate=pl.CostEstimate(
            flops=4 * frames * neurons * width,
            bytes_accessed=20 * 1024 * 1024,
            transcendentals=frames * neurons,
        ),
    )(
        spikes,
        row(held_in),
        readin_weight,
        qkv,
        out_weight,
        up_weight,
        down_weight,
        row(norm_gain),
        row(mlp_gain),
        row(final_gain),
        readout_weight,
        row(readout_bias),
    )
    latents, bits, total = pl.pallas_call(
        hand_over,
        out_shape=(
            jax.ShapeDtypeStruct((rows, width), BF),
            jax.ShapeDtypeStruct((1, neurons), F32),
            jax.ShapeDtypeStruct((1, 1), F32),
        ),
        in_specs=[vmem] * 3,
        out_specs=(vmem, vmem, vmem),
        compiler_params=pltpu.CompilerParams(vmem_limit_bytes=60 * 1024 * 1024),
    )(latents, bits, total)
    return latents, bits.reshape(neurons), total.reshape(())


def solution(mesh):
    in_specs = (
        P(None, ("neur", "tm")),
        P(("neur", "tm")),
        P(("neur", "tm"), None),
        P(None, None, "tm"),
        P("tm", None),
        P(None, "tm"),
        P("tm", None),
        P(),
        P(),
        P(),
        P(("neur", "tm"), None),
        P(("neur", "tm")),
    )
    out_specs = (P("neur", None), P(("neur", "tm")), P())
    return jax.shard_map(
        functools.partial(on_device, mesh.shape["neur"], mesh.shape["tm"]),
        mesh=mesh,
        in_specs=in_specs,
        out_specs=out_specs,
        check_vma=False,
    )
```
